32 devices in a mesh: grp: 2 (over y), keys: 4 (over x, core), qry: 4 (over z).
Axes of the slice: x: 2, y: 2, z: 4, core: 2. Of those that a mesh axis runs over, the one named last changes fastest.
Arguments:
- queries: bfloat16 [4096, 8, 128], P(('grp', 'keys', 'qry')), parts along dimension 0, may hold values from -40 to 40, as said below
- cache_keys: bfloat16 [4096, 128], P(('grp', 'keys')), parts along dimension 0, may hold values from -128 to 128, as said below
- cache_values: bfloat16 [4096, 128], P(('grp', 'keys')), parts along dimension 0, may hold values from -24 to 24
- entry: int32 [8, 4], P(('grp', 'keys'), 'qry'), parts along dimension 0, may hold values from 0 to 3
- visits: int32 [8, 4], P(('grp', 'keys'), 'qry'), parts along dimension 0, may hold values from 3 to 4
- doc_length: int32 [2], P('grp'), parts along dimension 0, may hold values from 1025 to 2048
- slot_params: float32 [2048, 256], P(('grp', 'keys', 'qry')), parts along dimension 0, may hold values from -128 to 128, as said below
- first_moment: float32 [2048, 256], P(('grp', 'keys', 'qry')), parts along dimension 0, may hold values from -3 to 3
- second_moment: float32 [2048, 256], P(('grp', 'keys', 'qry')), parts along dimension 0, may hold values from 0.05 to 1
Outputs:
- teacher_out: bfloat16 [4096, 8, 128], P(('grp', 'keys', 'qry')), parts along dimension 0
- slot_grad: float32 [2048, 256], P(('grp', 'keys', 'qry')), parts along dimension 0
- new_params: float32 [2048, 256], P(('grp', 'keys', 'qry')), parts along dimension 0
- new_first: float32 [2048, 256], P(('grp', 'keys', 'qry')), parts along dimension 0
- new_second: float32 [2048, 256], P(('grp', 'keys', 'qry')), parts along dimension 0
- loss: float32 [2], P('grp'), parts along dimension 0
The draws below stay inside these ranges and needn't reach their ends.
There are 2 independent parts, one for each index of `grp`. The reference program is written for one: setup_inputs(seed, part) draws one part's arguments, and reference() takes and returns one part's arrays. A program takes and returns all parts, laid end to end along the dimension named above; each array names one. Nothing has to cross between parts.
Inputs may be any that keep to these rules, and one draw needn't show every extreme that they name: `queries`: query entries stay within the stated range. `cache_keys`: cache key entries stay within the stated range. `slot_params`: slot entries stay within the stated range.
All inputs are finite; a program needn't handle non-finite values.
Results may differ from the reference program's by a relative error of at most 0.0045.
Values may be sent and summed in bfloat16 or wider, within the bound.
A program may use at most 64 MiB of HBM per device.

```python
import math
import jax
import jax.numpy as jnp
from jax import lax

HEADS = 8
HEAD_SIZE = 128
SLOTS = 1024
TOK_DEV = 128
CACHE_DEV = 512
TOKENS = 2048
CACHE = 2048
NBLK = 16
VMIN = 3
N_KEYS = 4
N_QRY = 4


def draw_queries(key, part):
    shape = (TOKENS, HEADS, HEAD_SIZE)
    base = jnp.clip(jax.random.normal(key, shape, jnp.float32), -6.0, 6.0)
    return base.astype(jnp.bfloat16)


def draw_cache_keys(key, part):
    shape = (CACHE, HEAD_SIZE)
    base = jnp.clip(2.0 * jax.random.normal(key, shape, jnp.float32), -12.0, 12.0)
    return base.astype(jnp.bfloat16)


def draw_slot_params(key, part):
    shape = (SLOTS, 2 * HEAD_SIZE)
    base = jnp.clip(jax.random.normal(key, shape, jnp.float32), -6.0, 6.0)
    return base


def touch_ends(drawn, rng, low, top_value):
    spot = [jax.random.randint(jax.random.fold_in(rng, axis), (), 0, length) for axis, length in enumerate(drawn.shape)]
    longest = drawn.shape.index(max(drawn.shape))
    next_to = spot[:longest] + [(spot[longest] + 1) % drawn.shape[longest]] + spot[longest + 1:]
    return drawn.at[tuple(spot)].set(low).at[tuple(next_to)].set(top_value)


def block_levels(stream_key, extent, pieces, low, largest):
    factor_of, own = 1.0, jax.random.fold_in(stream_key, 6)
    for axis_at, shards_of in pieces:
        draws = jnp.exp(jax.random.uniform(jax.random.fold_in(own, axis_at), (shards_of,), jnp.float32, low / len(pieces), largest / len(pieces)))
        factor_of = factor_of * jnp.repeat(draws, extent[axis_at] // shards_of).reshape([-1 if axis == axis_at else 1 for axis in range(len(extent))])
    return factor_of


def bell_draw(key, dims, deviation, most, split=(), kind=jnp.bfloat16):
    entries = jax.random.normal(key, dims, jnp.float32) * deviation
    if len(split) > 0:
        entries = block_levels(key, dims, split, -0.22, 0.18) * entries
    return jnp.clip(entries, min=-most, max=most).astype(kind)


def setup_inputs(seed: int = 0, part: int = 0) -> dict:
    arg_keys = jax.random.split(jax.random.key(seed), 10)
    part_keys = jax.random.split(jax.random.fold_in(arg_keys[9], part), 10)
    queries = draw_queries(jax.random.fold_in(jax.random.fold_in(arg_keys[9], part), 71), part)
    cache_keys = draw_cache_keys(jax.random.fold_in(jax.random.fold_in(arg_keys[9], part), 71), part)
    cache_values = bell_draw(part_keys[2], (CACHE, HEAD_SIZE), 4.0, 24.0, ((0, 4),))
    entry = touch_ends(jax.random.randint(part_keys[3], (N_KEYS, N_QRY), 0, N_KEYS), jax.random.fold_in(part_keys[3], 1), 0, N_KEYS - 1).astype(jnp.int32)
    visits = touch_ends(jax.random.randint(part_keys[4], (N_KEYS, N_QRY), VMIN, N_KEYS + 1), jax.random.fold_in(part_keys[4], 1), VMIN, N_KEYS).astype(jnp.int32)
    doc_length = jax.random.randint(part_keys[5], (1,), CACHE // 2 + 1, CACHE + 1).astype(jnp.int32)
    slot_params = draw_slot_params(jax.random.fold_in(jax.random.fold_in(arg_keys[9], part), 71), part)
    first_moment = bell_draw(part_keys[7], (SLOTS, 2 * HEAD_SIZE), 0.5, 3.0, ((0, 16),), jnp.float32)
    second_moment = jnp.clip(jnp.exp(math.log(1.0) - 2.9957323 * jax.random.uniform(part_keys[8], (SLOTS, 2 * HEAD_SIZE), jnp.float32) ** block_levels(part_keys[8], (SLOTS, 2 * HEAD_SIZE), ((0, 16),), -0.2, 0.2)), 0.05, 1.0)
    return dict(queries=queries, cache_keys=cache_keys, cache_values=cache_values, entry=entry, visits=visits, doc_length=doc_length, slot_params=slot_params, first_moment=first_moment, second_moment=second_moment)


NEG = -1e+30

def row_scores(left, right):
    return lax.dot_general(left, right, (((1,), (1,)), ((), ())), preferred_element_type=jnp.float32)

def student_tile(loop_state, block_entry, student_keys, student_values, score_scale):
    key_gradient, squared_terms = loop_state
    query_portion, target = block_entry
    logit_score = row_scores(query_portion, student_keys) * score_scale
    peak = lax.optimization_barrier(jnp.max(logit_score, axis=1, keepdims=True))
    weight = jnp.exp(logit_score - peak)
    prob = weight / lax.optimization_barrier(jnp.sum(weight, axis=1, keepdims=True))
    block_prob = prob.astype(jnp.bfloat16)
    student_output = jnp.dot(block_prob, student_values, preferred_element_type=jnp.float32)
    diff = student_output - target.astype(jnp.float32)
    squared_terms = squared_terms + jnp.sum(diff * diff)
    block_difference = diff.astype(jnp.bfloat16)
    prob_gradient = row_scores(block_difference, student_values)
    inner = lax.optimization_barrier(jnp.sum(prob * prob_gradient, axis=1, keepdims=True))
    dscore = (prob * (prob_gradient - inner) * score_scale).astype(jnp.bfloat16)
    dkeys = lax.dot_general(dscore, query_portion, (((0,), (0,)), ((), ())), preferred_element_type=jnp.float32)
    dvals = lax.dot_general(block_prob, block_difference, (((0,), (0,)), ((), ())), preferred_element_type=jnp.float32)
    key_gradient = key_gradient + jnp.concatenate([dkeys, dvals], axis=1)
    return ((key_gradient, squared_terms), None)

def reference(queries, cache_keys, cache_values, entry, visits, doc_length, slot_params, first_moment, second_moment):
    score_scale = 1.0 / math.sqrt(HEAD_SIZE)
    flat_entry = entry.reshape(-1)
    flat_visits = visits.reshape(-1)
    length = doc_length[0]

    def teacher_block(index):
        kidx = index // N_QRY
        start = flat_entry[index]
        count = flat_visits[index]
        query_portion = lax.dynamic_slice_in_dim(queries, (index * TOK_DEV).astype(jnp.int32), TOK_DEV, 0).reshape(TOK_DEV * HEADS, HEAD_SIZE)
        logit_score = row_scores(query_portion, cache_keys) * score_scale
        place = lax.iota(jnp.int32, CACHE)
        shard = place // CACHE_DEV
        live = (jnp.remainder(shard - kidx - start, N_KEYS) < count) & (place < length)
        live = live[None, :]
        logit_score = jnp.where(live, logit_score, NEG)
        peak = lax.optimization_barrier(jnp.max(logit_score, axis=1, keepdims=True))
        weight = jnp.where(live, jnp.exp(logit_score - peak), 0.0)
        total = lax.optimization_barrier(jnp.sum(weight, axis=1, keepdims=True))
        acc = jnp.dot(weight.astype(jnp.bfloat16), cache_values, preferred_element_type=jnp.float32)
        return (acc / total).astype(jnp.bfloat16).reshape(TOK_DEV, HEADS, HEAD_SIZE)
    teacher = lax.map(teacher_block, jnp.arange(NBLK, dtype=jnp.int32))
    teacher = teacher.reshape(TOKENS, HEADS, HEAD_SIZE)
    slot_replica = slot_params.astype(jnp.bfloat16)
    student_keys = slot_replica[:, :HEAD_SIZE]
    student_values = slot_replica[:, HEAD_SIZE:]
    rows = TOKENS * HEADS
    block = math.gcd(rows, 512)
    query_blocks = queries.reshape(rows // block, block, HEAD_SIZE)
    teacher_tiles = teacher.reshape(rows // block, block, HEAD_SIZE)
    initial_state = (jnp.zeros((SLOTS, 2 * HEAD_SIZE), jnp.float32), jnp.zeros((), jnp.float32))
    (key_gradient, squared_terms), ignored_value = lax.scan(lambda column_index, loop_index: student_tile(column_index, loop_index, student_keys, student_values, score_scale), initial_state, (query_blocks, teacher_tiles))
    new_first = 0.9 * first_moment + 0.1 * key_gradient
    new_second = 0.95 * second_moment + 0.05 * key_gradient * key_gradient
    new_params = slot_params - 0.02 * new_first / (jnp.sqrt(new_second) + 1e-08)
    loss = (squared_terms / rows).reshape(1)
    return (teacher, key_gradient, new_params, new_first, new_second, loss)
```

```python
import functools
import math

import jax
import jax.numpy as jnp
from jax import lax
from jax.experimental import pallas as pl
from jax.experimental.pallas import tpu as pltpu
from jax.sharding import PartitionSpec as P

NEG = -1e30


def shifted(block, axis, distance):
    devices = range(lax.axis_size(axis))
    route = [((i - distance) % len(devices), i) for i in devices]
    return lax.ppermute(block, axis, route)


def row_scores(left, right):
    return lax.dot_general(
        left, right, (((1,), (1,)), ((), ())), preferred_element_type=jnp.float32
    )


def attend(state, query_blocks, keys, values, shard, length, score_scale):
    block_width = keys.shape[0]
    place = shard * block_width + lax.iota(jnp.int32, block_width)
    live = (place < length)[None, :]

    def one(block_entry):
        query_portion, big, total, acc = block_entry
        logit_score = jnp.where(live, row_scores(query_portion, keys) * score_scale, NEG)
        new_big = jnp.maximum(big, jnp.max(logit_score, axis=1))
        weight = jnp.where(live, jnp.exp(logit_score - new_big[:, None]), 0.0)
        fade = jnp.exp(big - new_big)
        total = total * fade + jnp.sum(weight, axis=1)
        acc = acc * fade[:, None] + jnp.dot(
            weight.astype(jnp.bfloat16), values, preferred_element_type=jnp.float32
        )
        return (new_big, total, acc)

    big, total, acc = state
    return lax.map(one, (query_blocks, big, total, acc))


def student_tile(loop_state, block_entry, student_keys, student_values, score_scale):
    key_gradient, squared_terms = loop_state
    query_portion, target = block_entry
    logit_score = row_scores(query_portion, student_keys) * score_scale
    peak = jnp.max(logit_score, axis=1, keepdims=True)
    weight = jnp.exp(logit_score - peak)
    prob = weight / jnp.sum(weight, axis=1, keepdims=True)
    block_prob = prob.astype(jnp.bfloat16)
    student_output = jnp.dot(block_prob, student_values, preferred_element_type=jnp.float32)
    diff = student_output - target.astype(jnp.float32)
    squared_terms = squared_terms + jnp.sum(diff * diff)
    block_difference = diff.astype(jnp.bfloat16)
    prob_gradient = row_scores(block_difference, student_values)
    inner = jnp.sum(prob * prob_gradient, axis=1, keepdims=True)
    dscore = (prob * (prob_gradient - inner) * score_scale).astype(jnp.bfloat16)
    dkeys = lax.dot_general(
        dscore, query_portion, (((0,), (0,)), ((), ())), preferred_element_type=jnp.float32
    )
    dvals = lax.dot_general(
        block_prob, block_difference, (((0,), (0,)), ((), ())), preferred_element_type=jnp.float32
    )
    key_gradient = key_gradient + jnp.concatenate([dkeys, dvals], axis=1)
    return ((key_gradient, squared_terms), None)


def ringed(
    queries,
    cache_keys,
    cache_values,
    entry,
    visits,
    doc_length,
    slot_params,
    first_moment,
    second_moment,
):
    shards = lax.axis_size("keys")
    me = lax.axis_index("keys")
    tok, heads, block_width = queries.shape
    rows = tok * heads
    block = math.gcd(rows, 512)
    nblocks = rows // block
    score_scale = 1.0 / math.sqrt(block_width)
    length = doc_length[0]
    query_blocks = queries.reshape(nblocks, block, block_width)
    start = entry[0, 0]
    count = visits[0, 0]
    state = (
        jnp.full((nblocks, block), NEG, jnp.float32),
        jnp.zeros((nblocks, block), jnp.float32),
        jnp.zeros((nblocks, block, block_width), jnp.float32),
    )

    def visit(step, keys, values, loop_state):
        held = jnp.remainder(me - step, shards)
        go = jnp.remainder(-step - start, shards) < count
        return lax.cond(
            go,
            lambda column_index: attend(
                column_index, query_blocks, keys, values, held, length, score_scale
            ),
            lambda column_index: column_index,
            loop_state,
        )

    def turn(step, loop_state):
        keys, values, big, total, acc = loop_state
        big, total, acc = visit(step, keys, values, (big, total, acc))
        keys, values = shifted((keys, values), "keys", 1)
        return (keys, values, big, total, acc)

    keys, values, big, total, acc = lax.fori_loop(
        0, shards - 1, turn, (cache_keys, cache_values) + state
    )
    big, total, acc = visit(shards - 1, keys, values, (big, total, acc))
    teacher_block_list = (acc / total[:, :, None]).astype(jnp.bfloat16)
    teacher_out = teacher_block_list.reshape(tok, heads, block_width)
    copies = slot_params.astype(jnp.bfloat16)
    complete_sum = lax.all_gather(copies, ("keys", "qry"), axis=0, tiled=True)
    student_keys = complete_sum[:, :block_width]
    student_values = complete_sum[:, block_width:]
    initial_state = (jnp.zeros(complete_sum.shape, jnp.float32), jnp.zeros((), jnp.float32))
    (grad_terms, squared_terms), ignored_value = lax.scan(
        lambda column_index, loop_index: student_tile(
            column_index, loop_index, student_keys, student_values, score_scale
        ),
        initial_state,
        (query_blocks, teacher_block_list),
    )
    slot_grad = lax.psum_scatter(grad_terms, ("keys", "qry"), scatter_dimension=0, tiled=True)
    squares_all = lax.psum(squared_terms, ("keys", "qry"))
    loss = (squares_all / (rows * shards * lax.axis_size("qry"))).reshape(1)
    new_first = 0.9 * first_moment + 0.1 * slot_grad
    new_second = 0.95 * second_moment + 0.05 * slot_grad * slot_grad
    new_params = slot_params - 0.02 * new_first / (jnp.sqrt(new_second) + 1e-08)
    return (teacher_out, slot_grad, new_params, new_first, new_second, loss)


MESH = pl.DeviceIdType.MESH
LOW = -1e20
LOG2E = 1.4426950408889634


def pair_dot(left, right):
    return lax.dot_general(
        left, right, (((1,), (0,)), ((), ())), preferred_element_type=jnp.float32
    )


def step_kernel(
    n_keys,
    n_qry,
    entry_ref,
    visits_ref,
    length_ref,
    q_ref,
    k_ref,
    v_ref,
    slot_ref,
    first_ref,
    second_ref,
    teach_ref,
    grad_ref,
    params_ref,
    nfirst_ref,
    nsecond_ref,
    loss_ref,
    kbuf,
    vbuf,
    slots,
    top,
    acc,
    e_ref,
    pb_ref,
    ds_ref,
    student,
    diffb,
    gmine,
    gsib_out,
    gsib_in,
    gout,
    gin,
    sq_own,
    sq_sib,
    sq_chip,
    sq_in,
    kv_send,
    kv_recv,
    sl_send,
    sl_recv,
    gs_send,
    gs_recv,
    g_send,
    g_recv,
    sq_send,
    sq_recv,
):
    n_x = n_keys // 2
    n_flat = n_x * n_qry
    grp = lax.axis_index("grp")
    me_k = lax.axis_index("keys")
    me_q = lax.axis_index("qry")
    x = lax.div(me_k, 2)
    core = lax.rem(me_k, 2)
    flat = x * n_qry + me_q
    sibling = (grp, x * 2 + 1 - core, me_q)
    rows, width = q_ref.shape
    shard_len = k_ref.shape[0]
    per = slot_ref.shape[0]
    n_slots = slots.shape[0] * per
    scale = 1.0 / math.sqrt(width)
    rate = scale * LOG2E
    tile = math.gcd(rows, 256)
    tiles = rows // tile

    def place(f, c):
        return (lax.div(f, n_qry) * 2 + c) * n_qry + lax.rem(f, n_qry)

    def peer(f):
        return (grp, lax.div(f, n_qry) * 2 + core, lax.rem(f, n_qry))

    def ahead(o):
        return lax.rem(flat + o, n_flat)

    def behind(o):
        return lax.rem(flat + n_flat - o, n_flat)

    pending = []

    def send(src, dst, ssem, rsem, dev):
        copy = pltpu.make_async_remote_copy(
            src_ref=src, dst_ref=dst, send_sem=ssem, recv_sem=rsem,
            device_id=dev, device_id_type=MESH,
        )
        copy.start()
        pending.append(copy)

    def arrived(ref, ssem, rsem):
        pltpu.make_async_remote_copy(
            src_ref=ref, dst_ref=ref, send_sem=ssem, recv_sem=rsem,
            device_id=sibling, device_id_type=MESH,
        ).wait_recv()

    barrier = pltpu.get_barrier_semaphore()
    pl.semaphore_signal(barrier, inc=1, device_id=sibling, device_id_type=MESH)
    for o in range(1, n_flat):
        pl.semaphore_signal(barrier, inc=1, device_id=peer(ahead(o)), device_id_type=MESH)
    mine = place(flat, core)
    slots[mine] = slot_ref[...].astype(jnp.bfloat16)
    pl.semaphore_wait(barrier, n_flat)

    send(slots.at[mine], slots.at[mine], sl_send.at[0], sl_recv.at[0], sibling)
    send(k_ref, kbuf.at[0], kv_send.at[0], kv_recv.at[0], sibling)
    send(v_ref, vbuf.at[0], kv_send.at[1], kv_recv.at[1], sibling)
    for o in range(1, n_flat):
        send(slots.at[mine], slots.at[mine], sl_send.at[o], sl_recv.at[o], peer(ahead(o)))
    for j in range(1, n_x):
        there = (grp, lax.rem(x + j, n_x) * 2 + core, me_q)
        s = 2 * j - 1
        send(k_ref, kbuf.at[s], kv_send.at[2 * s], kv_recv.at[2 * s], there)
        send(v_ref, vbuf.at[s], kv_send.at[2 * s + 1], kv_recv.at[2 * s + 1], there)

    start = entry_ref[0, 0]
    count = visits_ref[0, 0]
    length = length_ref[0]
    ones = jnp.ones((shard_len, width), jnp.bfloat16)

    def attend(keys_ref, values_ref, shard, is_first):
        col = lax.broadcasted_iota(jnp.int32, (1, shard_len), 1) + shard * shard_len
        turn = lax.rem(shard - me_k - start + 2 * n_keys, n_keys)
        limit = jnp.where(turn < count, length, 0)
        bias = jnp.where(col < limit, 0.0, NEG)

        def one(t, carry):
            at = pl.ds(pl.multiple_of(t * tile, tile), tile)
            score = row_scores(q_ref[at, :], keys_ref[...]) + bias
            peak = jnp.max(score, axis=1, keepdims=True)
            values = jnp.concatenate([values_ref[...], ones], axis=1)
            if is_first:
                new = jnp.maximum(peak, LOW)
                weight = jnp.exp2((score - new) * rate)
                acc[at, :] = pair_dot(weight.astype(jnp.bfloat16), values)
            else:
                old = top[at, 0:1]
                new = jnp.maximum(peak, old)
                weight = jnp.exp2((score - new) * rate)
                fade = jnp.exp2((old - new) * rate)
                acc[at, :] = acc[at, :] * fade + pair_dot(weight.astype(jnp.bfloat16), values)
            top[at, :] = jnp.broadcast_to(new, (tile, width))
            return carry

        lax.fori_loop(0, tiles, one, 0, unroll=2)

    attend(k_ref, v_ref, me_k, True)
    arrived(kbuf.at[0], kv_send.at[0], kv_recv.at[0])
    arrived(vbuf.at[0], kv_send.at[1], kv_recv.at[1])
    attend(kbuf.at[0], vbuf.at[0], x * 2 + 1 - core, False)

    for o in range(1, n_flat):
        block = place(behind(o), core)
        arrived(slots.at[block], sl_send.at[o], sl_recv.at[o])
        i = n_flat - 1 + o
        send(slots.at[block], slots.at[block], sl_send.at[i], sl_recv.at[i], sibling)
    arrived(slots.at[place(flat, 1 - core)], sl_send.at[0], sl_recv.at[0])
    for o in range(1, n_flat):
        i = n_flat - 1 + o
        arrived(slots.at[place(behind(o), 1 - core)], sl_send.at[i], sl_recv.at[i])

    def slot_keys():
        return slots[:, :, 0:width].reshape(n_slots, width)

    def slot_values():
        return slots[:, :, width:].reshape(n_slots, width)

    def grouped(value):
        return value.reshape(slots.shape[0], per, tile)

    values_t = slot_values().astype(jnp.float32).T.astype(jnp.bfloat16)

    def softmax(t, carry):
        at = pl.ds(pl.multiple_of(t * tile, tile), tile)
        score = row_scores(slot_keys(), q_ref[at, :])
        peak = jnp.max(score, axis=0, keepdims=True)
        weight = jnp.exp2((score - peak) * rate)
        prob = weight * (1.0 / jnp.sum(weight, axis=0, keepdims=True))
        e_ref[:, :, at] = grouped(prob)
        prob_b = prob.astype(jnp.bfloat16)
        pb_ref[:, :, at] = grouped(prob_b)
        student[at, :] = pair_dot(values_t, prob_b).T
        return carry

    lax.fori_loop(0, tiles, softmax, 0)

    for j in range(1, n_x):
        s = 2 * j - 1
        arrived(kbuf.at[s], kv_send.at[2 * s], kv_recv.at[2 * s])
        arrived(vbuf.at[s], kv_send.at[2 * s + 1], kv_recv.at[2 * s + 1])
        g = s + 1
        send(kbuf.at[s], kbuf.at[g], kv_send.at[2 * g], kv_recv.at[2 * g], sibling)
        send(vbuf.at[s], vbuf.at[g], kv_send.at[2 * g + 1], kv_recv.at[2 * g + 1], sibling)
    for j in range(1, n_x):
        far = lax.rem(x + n_x - j, n_x) * 2
        s = 2 * j - 1
        attend(kbuf.at[s], vbuf.at[s], far + core, False)
        g = s + 1
        arrived(kbuf.at[g], kv_send.at[2 * g], kv_recv.at[2 * g])
        arrived(vbuf.at[g], kv_send.at[2 * g + 1], kv_recv.at[2 * g + 1])
        attend(kbuf.at[g], vbuf.at[g], far + 1 - core, False)

    sq_own[...] = jnp.zeros_like(sq_own)

    def differ(t, carry):
        at = pl.ds(pl.multiple_of(t * tile, tile), tile)
        teacher = (acc[at, 0:width] / acc[at, width:]).astype(jnp.bfloat16)
        teach_ref[at, :] = teacher
        diff = student[at, :] - teacher.astype(jnp.float32)
        sq_own[...] += jnp.sum((diff * diff).reshape(tile // 8, 8, width), axis=0)
        diff_b = diff.astype(jnp.bfloat16)
        diffb[at, :] = diff_b
        dprob = row_scores(slot_values(), diff_b)
        prob = e_ref[:, :, at].reshape(n_slots, tile)
        inner = jnp.sum(prob * dprob, axis=0, keepdims=True)
        ds_ref[:, :, at] = grouped((prob * (dprob - inner) * scale).astype(jnp.bfloat16))
        return carry

    lax.fori_loop(0, tiles, differ, 0)
    send(sq_own, sq_sib, sq_send.at[0], sq_recv.at[0], sibling)

    order = list(range(1, n_flat)) + [0]
    group = 2 if n_flat % 2 == 0 else 1
    batches = [order[i:i + group] for i in range(0, n_flat, group)]

    def produce(batch):
        blocks = []
        for o in batch:
            blocks += [place(ahead(o), 1 - core), place(ahead(o), core)]
        dkeys = pair_dot(jnp.concatenate([ds_ref[b] for b in blocks], axis=0), q_ref[...])
        dvals = pair_dot(jnp.concatenate([pb_ref[b] for b in blocks], axis=0), diffb[...])
        for i, o in enumerate(batch):
            a = 2 * i * per
            gsib_out[o, :, 0:width] = dkeys[a:a + per]
            gsib_out[o, :, width:] = dvals[a:a + per]
            send(gsib_out.at[o], gsib_in.at[o], gs_send.at[o], gs_recv.at[o], sibling)
            gmine[o, :, 0:width] = dkeys[a + per:a + 2 * per]
            gmine[o, :, width:] = dvals[a + per:a + 2 * per]

    def finish(batch):
        for o in batch:
            arrived(gsib_in.at[o], gs_send.at[o], gs_recv.at[o])
            if o > 0:
                gout[o] = (gmine[o] + gsib_in[o]).astype(jnp.bfloat16)
                send(gout.at[o], gin.at[o], g_send.at[o], g_recv.at[o], peer(ahead(o)))

    for i, batch in enumerate(batches):
        produce(batch)
        if i > 0:
            finish(batches[i - 1])
        if i == 0:
            arrived(sq_sib, sq_send.at[0], sq_recv.at[0])
            sq_chip[...] = sq_own[...] + sq_sib[...]
            for o in range(1, n_flat):
                send(sq_chip, sq_in.at[o], sq_send.at[o], sq_recv.at[o], peer(ahead(o)))
    finish(batches[-1])

    total = gmine[0] + gsib_in[0]
    squares = sq_chip[...]
    for o in range(1, n_flat):
        arrived(sq_in.at[o], sq_send.at[o], sq_recv.at[o])
        squares = squares + sq_in[o]
    loss_ref[0] = jnp.sum(squares) * (1.0 / (rows * n_keys * n_qry))
    for o in range(1, n_flat):
        arrived(gin.at[o], g_send.at[o], g_recv.at[o])
        total = total + gin[o].astype(jnp.float32)
    new_first = 0.9 * first_ref[...] + 0.1 * total
    new_second = 0.95 * second_ref[...] + 0.05 * total * total
    grad_ref[...] = total
    nfirst_ref[...] = new_first
    nsecond_ref[...] = new_second
    params_ref[...] = slot_ref[...] - 0.02 * new_first / (jnp.sqrt(new_second) + 1e-08)
    for copy in pending:
        copy.wait_send()


def fused(
    queries, cache_keys, cache_values, entry, visits, doc_length, slot_params,
    first_moment, second_moment,
):
    n_keys = lax.axis_size("keys")
    n_qry = lax.axis_size("qry")
    n_flat = n_keys // 2 * n_qry
    n_blocks = n_keys * n_qry
    tok, heads, width = queries.shape
    rows = tok * heads
    per, wide = slot_params.shape
    shard_len = cache_keys.shape[0]
    n_slots = per * n_blocks
    f32, bf16 = jnp.float32, jnp.bfloat16
    vmem = pl.BlockSpec(memory_space=pltpu.VMEM)
    smem = pl.BlockSpec(memory_space=pltpu.SMEM)
    dma = pltpu.SemaphoreType.DMA
    owned = jax.ShapeDtypeStruct((per, wide), f32)
    flops = 2 * rows * width * (2 * n_keys * shard_len + 5 * n_slots)
    out = pl.pallas_call(
        functools.partial(step_kernel, n_keys, n_qry),
        out_shape=(
            jax.ShapeDtypeStruct((rows, width), bf16),
            owned, owned, owned, owned,
            jax.ShapeDtypeStruct((1,), f32),
        ),
        in_specs=[smem] * 3 + [vmem] * 6,
        out_specs=(vmem,) * 5 + (smem,),
        scratch_shapes=[
            pltpu.VMEM((n_keys - 1, shard_len, width), bf16),
            pltpu.VMEM((n_keys - 1, shard_len, width), bf16),
            pltpu.VMEM((n_blocks, per, wide), bf16),
            pltpu.VMEM((rows, width), f32),
            pltpu.VMEM((rows, 2 * width), f32),
            pltpu.VMEM((n_blocks, per, rows), f32),
            pltpu.VMEM((n_blocks, per, rows), bf16),
            pltpu.VMEM((n_blocks, per, rows), bf16),
            pltpu.VMEM((rows, width), f32),
            pltpu.VMEM((rows, width), bf16),
            pltpu.VMEM((n_flat, per, wide), f32),
            pltpu.VMEM((n_flat, per, wide), f32),
            pltpu.VMEM((n_flat, per, wide), f32),
            pltpu.VMEM((n_flat, per, wide), bf16),
            pltpu.VMEM((n_flat, per, wide), bf16),
            pltpu.VMEM((8, width), f32),
            pltpu.VMEM((8, width), f32),
            pltpu.VMEM((8, width), f32),
            pltpu.VMEM((n_flat, 8, width), f32),
            dma((2 * (n_keys - 1),)),
            dma((2 * (n_keys - 1),)),
            dma((2 * n_flat - 1,)),
            dma((2 * n_flat - 1,)),
            dma((n_flat,)),
            dma((n_flat,)),
            dma((n_flat,)),
            dma((n_flat,)),
            dma((n_flat,)),
            dma((n_flat,)),
        ],
        compiler_params=pltpu.CompilerParams(
            collective_id=0, has_side_effects=True, vmem_limit_bytes=48 * 2**20
        ),
        cost_estimate=pl.CostEstimate(
            flops=flops, bytes_accessed=4 * rows * width, transcendentals=rows * n_slots
        ),
    )(
        entry, visits, doc_length, queries.reshape(rows, width), cache_keys, cache_values,
        slot_params, first_moment, second_moment,
    )
    return (out[0].reshape(tok, heads, width),) + tuple(out[1:])


def body(*args):
    per = args[6].shape[0]
    if per % 16 == 0 and lax.axis_size("keys") % 2 == 0:
        return fused(*args)
    return ringed(*args)


def solution(mesh):
    return jax.shard_map(
        body,
        mesh=mesh,
        in_specs=(
            P(("grp", "keys", "qry"), None, None),
            P(("grp", "keys"), None),
            P(("grp", "keys"), None),
            P(("grp", "keys"), "qry"),
            P(("grp", "keys"), "qry"),
            P("grp"),
            P(("grp", "keys", "qry"), None),
            P(("grp", "keys", "qry"), None),
            P(("grp", "keys", "qry"), None),
        ),
        out_specs=(
            P(("grp", "keys", "qry"), None, None),
            P(("grp", "keys", "qry"), None),
            P(("grp", "keys", "qry"), None),
            P(("grp", "keys", "qry"), None),
            P(("grp", "keys", "qry"), None),
            P("grp"),
        ),
        check_vma=False,
    )
```

```python
import functools
import math

import jax
import jax.numpy as jnp
from jax import lax
from jax.experimental import pallas as pl
from jax.experimental.pallas import tpu as pltpu
from jax.sharding import PartitionSpec as P

NEG = -1e30


def shifted(block, axis, distance):
    devices = range(lax.axis_size(axis))
    route = [((i - distance) % len(devices), i) for i in devices]
    return lax.ppermute(block, axis, route)


def row_scores(left, right):
    return lax.dot_general(
        left, right, (((1,), (1,)), ((), ())), preferred_element_type=jnp.float32
    )


def attend(state, query_blocks, keys, values, shard, length, score_scale):
    block_width = keys.shape[0]
    place = shard * block_width + lax.iota(jnp.int32, block_width)
    live = (place < length)[None, :]

    def one(block_entry):
        query_portion, big, total, acc = block_entry
        logit_score = jnp.where(live, row_scores(query_portion, keys) * score_scale, NEG)
        new_big = jnp.maximum(big, jnp.max(logit_score, axis=1))
        weight = jnp.where(live, jnp.exp(logit_score - new_big[:, None]), 0.0)
        fade = jnp.exp(big - new_big)
        total = total * fade + jnp.sum(weight, axis=1)
        acc = acc * fade[:, None] + jnp.dot(
            weight.astype(jnp.bfloat16), values, preferred_element_type=jnp.float32
        )
        return (new_big, total, acc)

    big, total, acc = state
    return lax.map(one, (query_blocks, big, total, acc))


def student_tile(loop_state, block_entry, student_keys, student_values, score_scale):
    key_gradient, squared_terms = loop_state
    query_portion, target = block_entry
    logit_score = row_scores(query_portion, student_keys) * score_scale
    peak = jnp.max(logit_score, axis=1, keepdims=True)
    weight = jnp.exp(logit_score - peak)
    prob = weight / jnp.sum(weight, axis=1, keepdims=True)
    block_prob = prob.astype(jnp.bfloat16)
    student_output = jnp.dot(block_prob, student_values, preferred_element_type=jnp.float32)
    diff = student_output - target.astype(jnp.float32)
    squared_terms = squared_terms + jnp.sum(diff * diff)
    block_difference = diff.astype(jnp.bfloat16)
    prob_gradient = row_scores(block_difference, student_values)
    inner = jnp.sum(prob * prob_gradient, axis=1, keepdims=True)
    dscore = (prob * (prob_gradient - inner) * score_scale).astype(jnp.bfloat16)
    dkeys = lax.dot_general(
        dscore, query_portion, (((0,), (0,)), ((), ())), preferred_element_type=jnp.float32
    )
    dvals = lax.dot_general(
        block_prob, block_difference, (((0,), (0,)), ((), ())), preferred_element_type=jnp.float32
    )
    key_gradient = key_gradient + jnp.concatenate([dkeys, dvals], axis=1)
    return ((key_gradient, squared_terms), None)


def ringed(
    queries,
    cache_keys,
    cache_values,
    entry,
    visits,
    doc_length,
    slot_params,
    first_moment,
    second_moment,
):
    shards = lax.axis_size("keys")
    me = lax.axis_index("keys")
    tok, heads, block_width = queries.shape
    rows = tok * heads
    block = math.gcd(rows, 512)
    nblocks = rows // block
    score_scale = 1.0 / math.sqrt(block_width)
    length = doc_length[0]
    query_blocks = queries.reshape(nblocks, block, block_width)
    start = entry[0, 0]
    count = visits[0, 0]
    state = (
        jnp.full((nblocks, block), NEG, jnp.float32),
        jnp.zeros((nblocks, block), jnp.float32),
        jnp.zeros((nblocks, block, block_width), jnp.float32),
    )

    def visit(step, keys, values, loop_state):
        held = jnp.remainder(me - step, shards)
        go = jnp.remainder(-step - start, shards) < count
        return lax.cond(
            go,
            lambda column_index: attend(
                column_index, query_blocks, keys, values, held, length, score_scale
            ),
            lambda column_index: column_index,
            loop_state,
        )

    def turn(step, loop_state):
        keys, values, big, total, acc = loop_state
        big, total, acc = visit(step, keys, values, (big, total, acc))
        keys, values = shifted((keys, values), "keys", 1)
        return (keys, values, big, total, acc)

    keys, values, big, total, acc = lax.fori_loop(
        0, shards - 1, turn, (cache_keys, cache_values) + state
    )
    big, total, acc = visit(shards - 1, keys, values, (big, total, acc))
    teacher_block_list = (acc / total[:, :, None]).astype(jnp.bfloat16)
    teacher_out = teacher_block_list.reshape(tok, heads, block_width)
    copies = slot_params.astype(jnp.bfloat16)
    complete_sum = lax.all_gather(copies, ("keys", "qry"), axis=0, tiled=True)
    student_keys = complete_sum[:, :block_width]
    student_values = complete_sum[:, block_width:]
    initial_state = (jnp.zeros(complete_sum.shape, jnp.float32), jnp.zeros((), jnp.float32))
    (grad_terms, squared_terms), ignored_value = lax.scan(
        lambda column_index, loop_index: student_tile(
            column_index, loop_index, student_keys, student_values, score_scale
        ),
        initial_state,
        (query_blocks, teacher_block_list),
    )
    slot_grad = lax.psum_scatter(grad_terms, ("keys", "qry"), scatter_dimension=0, tiled=True)
    squares_all = lax.psum(squared_terms, ("keys", "qry"))
    loss = (squares_all / (rows * shards * lax.axis_size("qry"))).reshape(1)
    new_first = 0.9 * first_moment + 0.1 * slot_grad
    new_second = 0.95 * second_moment + 0.05 * slot_grad * slot_grad
    new_params = slot_params - 0.02 * new_first / (jnp.sqrt(new_second) + 1e-08)
    return (teacher_out, slot_grad, new_params, new_first, new_second, loss)


MESH = pl.DeviceIdType.MESH
LOW = -1e20
LOG2E = 1.4426950408889634


def pair_dot(left, right):
    return lax.dot_general(
        left, right, (((1,), (0,)), ((), ())), preferred_element_type=jnp.float32
    )


def step_kernel(
    n_keys,
    n_qry,
    entry_ref,
    visits_ref,
    length_ref,
    q_hbm,
    k_hbm,
    v_hbm,
    slot_hbm,
    first_hbm,
    second_hbm,
    teach_hbm,
    owned_hbm,
    loss_ref,
    teach_ref,
    owned_ref,
    q_ref,
    k_ref,
    v_ref,
    slot_ref,
    first_ref,
    second_ref,
    kbuf,
    vbuf,
    slots,
    top,
    acc,
    e_ref,
    pb_ref,
    ds_ref,
    student,
    diffb,
    gmine,
    gsib_out,
    gsib_in,
    gout,
    gin,
    sq_own,
    sq_sib,
    sq_chip,
    sq_in,
    in_sem,
    out_sem,
    kv_send,
    kv_recv,
    sl_send,
    sl_recv,
    gs_send,
    gs_recv,
    g_send,
    g_recv,
    sq_send,
    sq_recv,
):
    n_x = n_keys // 2
    n_flat = n_x * n_qry
    grp = lax.axis_index("grp")
    me_k = lax.axis_index("keys")
    me_q = lax.axis_index("qry")
    x = lax.div(me_k, 2)
    core = lax.rem(me_k, 2)
    flat = x * n_qry + me_q
    sibling = (grp, x * 2 + 1 - core, me_q)
    rows, width = q_ref.shape
    shard_len = k_ref.shape[0]
    per = slot_ref.shape[0]
    n_slots = slots.shape[0] * per
    scale = 1.0 / math.sqrt(width)
    rate = scale * LOG2E
    tile = math.gcd(rows, 256)
    tiles = rows // tile

    def place(f, c):
        return (lax.div(f, n_qry) * 2 + c) * n_qry + lax.rem(f, n_qry)

    def peer(f):
        return (grp, lax.div(f, n_qry) * 2 + core, lax.rem(f, n_qry))

    def ahead(o):
        return lax.rem(flat + o, n_flat)

    def behind(o):
        return lax.rem(flat + n_flat - o, n_flat)

    pending = []

    def send(src, dst, ssem, rsem, dev):
        copy = pltpu.make_async_remote_copy(
            src_ref=src, dst_ref=dst, send_sem=ssem, recv_sem=rsem,
            device_id=dev, device_id_type=MESH,
        )
        copy.start()
        pending.append(copy)

    def arrived(ref, ssem, rsem):
        pltpu.make_async_remote_copy(
            src_ref=ref, dst_ref=ref, send_sem=ssem, recv_sem=rsem,
            device_id=sibling, device_id_type=MESH,
        ).wait_recv()

    loads = [
        pltpu.make_async_copy(src, dst, in_sem.at[i])
        for i, (src, dst) in enumerate((
            (slot_hbm, slot_ref), (q_hbm, q_ref), (k_hbm, k_ref), (v_hbm, v_ref),
            (first_hbm, first_ref), (second_hbm, second_ref),
        ))
    ]
    for load in loads:
        load.start()

    barrier = pltpu.get_barrier_semaphore()
    pl.semaphore_signal(barrier, inc=1, device_id=sibling, device_id_type=MESH)
    for o in range(1, n_flat):
        pl.semaphore_signal(barrier, inc=1, device_id=peer(ahead(o)), device_id_type=MESH)
    mine = place(flat, core)
    loads[0].wait()
    slots[mine] = slot_ref[...].astype(jnp.bfloat16)
    pl.semaphore_wait(barrier, n_flat)

    send(slots.at[mine], slots.at[mine], sl_send.at[0], sl_recv.at[0], sibling)
    send(k_hbm, kbuf.at[0], kv_send.at[0], kv_recv.at[0], sibling)
    send(v_hbm, vbuf.at[0], kv_send.at[1], kv_recv.at[1], sibling)
    for o in range(1, n_flat):
        send(slots.at[mine], slots.at[mine], sl_send.at[o], sl_recv.at[o], peer(ahead(o)))
    for j in range(1, n_x):
        there = (grp, lax.rem(x + j, n_x) * 2 + core, me_q)
        s = 2 * j - 1
        send(k_hbm, kbuf.at[s], kv_send.at[2 * s], kv_recv.at[2 * s], there)
        send(v_hbm, vbuf.at[s], kv_send.at[2 * s + 1], kv_recv.at[2 * s + 1], there)

    start = entry_ref[0, 0]
    count = visits_ref[0, 0]
    length = length_ref[0]
    ones = jnp.ones((shard_len, width), jnp.bfloat16)

    def attend(keys_ref, values_ref, shard, is_first):
        col = lax.broadcasted_iota(jnp.int32, (1, shard_len), 1) + shard * shard_len
        turn = lax.rem(shard - me_k - start + 2 * n_keys, n_keys)
        limit = jnp.where(turn < count, length, 0)
        bias = jnp.where(col < limit, 0.0, NEG)

        def one(t, carry):
            at = pl.ds(pl.multiple_of(t * tile, tile), tile)
            score = row_scores(q_ref[at, :], keys_ref[...]) + bias
            peak = jnp.max(score, axis=1, keepdims=True)
            values = jnp.concatenate([values_ref[...], ones], axis=1)
            if is_first:
                new = jnp.maximum(peak, LOW)
                weight = jnp.exp2((score - new) * rate)
                acc[at, :] = pair_dot(weight.astype(jnp.bfloat16), values)
            else:
                old = top[at, 0:1]
                new = jnp.maximum(peak, old)
                weight = jnp.exp2((score - new) * rate)
                fade = jnp.exp2((old - new) * rate)
                acc[at, :] = acc[at, :] * fade + pair_dot(weight.astype(jnp.bfloat16), values)
            top[at, :] = jnp.broadcast_to(new, (tile, width))
            return carry

        lax.fori_loop(0, tiles, one, 0, unroll=2)

    for load in loads[1:4]:
        load.wait()
    attend(k_ref, v_ref, me_k, True)
    arrived(kbuf.at[0], kv_send.at[0], kv_recv.at[0])
    arrived(vbuf.at[0], kv_send.at[1], kv_recv.at[1])
    attend(kbuf.at[0], vbuf.at[0], x * 2 + 1 - core, False)

    for o in range(1, n_flat):
        block = place(behind(o), core)
        arrived(slots.at[block], sl_send.at[o], sl_recv.at[o])
        i = n_flat - 1 + o
        send(slots.at[block], slots.at[block], sl_send.at[i], sl_recv.at[i], sibling)
    arrived(slots.at[place(flat, 1 - core)], sl_send.at[0], sl_recv.at[0])
    for o in range(1, n_flat):
        i = n_flat - 1 + o
        arrived(slots.at[place(behind(o), 1 - core)], sl_send.at[i], sl_recv.at[i])

    def slot_keys():
        return slots[:, :, 0:width].reshape(n_slots, width)

    def slot_values():
        return slots[:, :, width:].reshape(n_slots, width)

    def grouped(value):
        return value.reshape(slots.shape[0], per, tile)

    values_t = slot_values().astype(jnp.float32).T.astype(jnp.bfloat16)

    def softmax(t, carry):
        at = pl.ds(pl.multiple_of(t * tile, tile), tile)
        score = row_scores(slot_keys(), q_ref[at, :])
        peak = jnp.max(score, axis=0, keepdims=True)
        weight = jnp.exp2((score - peak) * rate)
        prob = weight * (1.0 / jnp.sum(weight, axis=0, keepdims=True))
        e_ref[:, :, at] = grouped(prob)
        prob_b = prob.astype(jnp.bfloat16)
        pb_ref[:, :, at] = grouped(prob_b)
        student[at, :] = pair_dot(values_t, prob_b).T
        return carry

    lax.fori_loop(0, tiles, softmax, 0)

    for j in range(1, n_x):
        s = 2 * j - 1
        arrived(kbuf.at[s], kv_send.at[2 * s], kv_recv.at[2 * s])
        arrived(vbuf.at[s], kv_send.at[2 * s + 1], kv_recv.at[2 * s + 1])
        g = s + 1
        send(kbuf.at[s], kbuf.at[g], kv_send.at[2 * g], kv_recv.at[2 * g], sibling)
        send(vbuf.at[s], vbuf.at[g], kv_send.at[2 * g + 1], kv_recv.at[2 * g + 1], sibling)
    for j in range(1, n_x):
        far = lax.rem(x + n_x - j, n_x) * 2
        s = 2 * j - 1
        attend(kbuf.at[s], vbuf.at[s], far + core, False)
        g = s + 1
        arrived(kbuf.at[g], kv_send.at[2 * g], kv_recv.at[2 * g])
        arrived(vbuf.at[g], kv_send.at[2 * g + 1], kv_recv.at[2 * g + 1])
        attend(kbuf.at[g], vbuf.at[g], far + 1 - core, False)

    sq_own[...] = jnp.zeros_like(sq_own)
    for t in range(tiles):
        at = pl.ds(t * tile, tile)
        teacher = (acc[at, 0:width] / acc[at, width:]).astype(jnp.bfloat16)
        teach_ref[at, :] = teacher
        diff = student[at, :] - teacher.astype(jnp.float32)
        sq_own[...] += jnp.sum((diff * diff).reshape(tile // 8, 8, width), axis=0)
        diffb[at, :] = diff.astype(jnp.bfloat16)
    write_teach = pltpu.make_async_copy(teach_ref, teach_hbm, out_sem.at[0])
    write_teach.start()
    send(sq_own, sq_sib, sq_send.at[0], sq_recv.at[0], sibling)

    order = list(range(1, n_flat)) + [0]
    group = 2 if n_flat % 2 == 0 else 1
    batches = n_flat // group
    VALUES, KEYS = 0, 1

    def produce(half, i):
        left, right = ((pb_ref, diffb), (ds_ref, q_ref))[half]
        first = i * group
        offsets = order[first:first + group]
        blocks = [place(ahead(o), 1 - core) for o in offsets]
        blocks += [place(ahead(o), core) for o in offsets]
        terms = pair_dot(jnp.concatenate([left[b] for b in blocks], axis=0), right[...])
        terms = terms.reshape(2, group, per, width)
        span = pl.ds(first, group)
        gsib_out[half, span] = terms[0]
        gmine[half, span] = terms[1]
        sem = half * batches + i
        send(gsib_out.at[half, span], gsib_in.at[half, span], gs_send.at[sem], gs_recv.at[sem], sibling)

    def finish(half, i):
        first = i * group
        sem = half * batches + i
        arrived(gsib_in.at[half, pl.ds(first, group)], gs_send.at[sem], gs_recv.at[sem])
        for p in range(first, first + group):
            o = order[p]
            if o > 0:
                gout[half, p] = (gmine[half, p] + gsib_in[half, p]).astype(jnp.bfloat16)
                i = half * n_flat + p
                send(gout.at[half, p], gin.at[half, p], g_send.at[i], g_recv.at[i], peer(ahead(o)))

    for i in range(batches):
        produce(VALUES, i)
        if i > 0:
            finish(VALUES, i - 1)
    finish(VALUES, batches - 1)
    arrived(sq_sib, sq_send.at[0], sq_recv.at[0])
    sq_chip[...] = sq_own[...] + sq_sib[...]
    for o in range(1, n_flat):
        send(sq_chip, sq_in.at[o], sq_send.at[o], sq_recv.at[o], peer(ahead(o)))

    for t in range(tiles):
        at = pl.ds(t * tile, tile)
        dprob = row_scores(slot_values(), diffb[at, :])
        prob = e_ref[:, :, at].reshape(n_slots, tile)
        inner = jnp.sum(prob * dprob, axis=0, keepdims=True)
        ds_ref[:, :, at] = grouped((prob * (dprob - inner) * scale).astype(jnp.bfloat16))

    for i in range(batches):
        produce(KEYS, i)
        if i > 0:
            finish(KEYS, i - 1)
    finish(KEYS, batches - 1)

    squares = sq_chip[...]
    for o in range(1, n_flat):
        arrived(sq_in.at[o], sq_send.at[o], sq_recv.at[o])
        squares = squares + sq_in[o]
    loss_ref[0] = jnp.sum(squares) * (1.0 / (rows * n_keys * n_qry))
    for load in loads[4:]:
        load.wait()
    for half in (VALUES, KEYS):
        total = gmine[half, n_flat - 1] + gsib_in[half, n_flat - 1]
        for p in range(n_flat - 1):
            i = half * n_flat + p
            arrived(gin.at[half, p], g_send.at[i], g_recv.at[i])
            total = total + gin[half, p].astype(jnp.float32)
        part = pl.ds(width if half == VALUES else 0, width)
        new_first = 0.9 * first_ref[:, part] + 0.1 * total
        new_second = 0.95 * second_ref[:, part] + 0.05 * total * total
        owned_ref[0, :, part] = total
        owned_ref[1, :, part] = slot_ref[:, part] - 0.02 * new_first / (jnp.sqrt(new_second) + 1e-08)
        owned_ref[2, :, part] = new_first
        owned_ref[3, :, part] = new_second
    write_owned = pltpu.make_async_copy(owned_ref, owned_hbm, out_sem.at[1])
    write_owned.start()
    write_teach.wait()
    write_owned.wait()
    for copy in pending:
        copy.wait_send()


def write_kernel(teach_ref, owned_ref, teach_out, grad_out, params_out, first_out, second_out, sems):
    copies = [pltpu.make_async_copy(teach_ref, teach_out, sems.at[4])]
    for i, out in enumerate((grad_out, params_out, first_out, second_out)):
        copies.append(pltpu.make_async_copy(owned_ref.at[i], out, sems.at[i]))
    for copy in copies:
        copy.start()
    for copy in copies:
        copy.wait()


def fused(
    queries, cache_keys, cache_values, entry, visits, doc_length, slot_params,
    first_moment, second_moment,
):
    n_keys = lax.axis_size("keys")
    n_qry = lax.axis_size("qry")
    n_flat = n_keys // 2 * n_qry
    n_blocks = n_keys * n_qry
    tok, heads, width = queries.shape
    rows = tok * heads
    per, wide = slot_params.shape
    shard_len = cache_keys.shape[0]
    n_slots = per * n_blocks
    f32, bf16 = jnp.float32, jnp.bfloat16
    hbm = pl.BlockSpec(memory_space=pltpu.HBM)
    smem = pl.BlockSpec(memory_space=pltpu.SMEM)
    dma = pltpu.SemaphoreType.DMA
    owned = jax.ShapeDtypeStruct((per, wide), f32)
    flops = 2 * rows * width * (2 * n_keys * shard_len + 5 * n_slots)
    teach, stacked, loss = pl.pallas_call(
        functools.partial(step_kernel, n_keys, n_qry),
        out_shape=(
            jax.ShapeDtypeStruct((rows, width), bf16),
            jax.ShapeDtypeStruct((4, per, wide), f32),
            jax.ShapeDtypeStruct((1,), f32),
        ),
        in_specs=[smem] * 3 + [hbm] * 6,
        out_specs=(hbm, hbm, smem),
        scratch_shapes=[
            pltpu.VMEM((rows, width), bf16),
            pltpu.VMEM((4, per, wide), f32),
            pltpu.VMEM((rows, width), bf16),
            pltpu.VMEM((shard_len, width), bf16),
            pltpu.VMEM((shard_len, width), bf16),
            pltpu.VMEM((per, wide), f32),
            pltpu.VMEM((per, wide), f32),
            pltpu.VMEM((per, wide), f32),
            pltpu.VMEM((n_keys - 1, shard_len, width), bf16),
            pltpu.VMEM((n_keys - 1, shard_len, width), bf16),
            pltpu.VMEM((n_blocks, per, wide), bf16),
            pltpu.VMEM((rows, width), f32),
            pltpu.VMEM((rows, 2 * width), f32),
            pltpu.VMEM((n_blocks, per, rows), f32),
            pltpu.VMEM((n_blocks, per, rows), bf16),
            pltpu.VMEM((n_blocks, per, rows), bf16),
            pltpu.VMEM((rows, width), f32),
            pltpu.VMEM((rows, width), bf16),
            pltpu.VMEM((2, n_flat, per, width), f32),
            pltpu.VMEM((2, n_flat, per, width), f32),
            pltpu.VMEM((2, n_flat, per, width), f32),
            pltpu.VMEM((2, n_flat, per, width), bf16),
            pltpu.VMEM((2, n_flat, per, width), bf16),
            pltpu.VMEM((8, width), f32),
            pltpu.VMEM((8, width), f32),
            pltpu.VMEM((8, width), f32),
            pltpu.VMEM((n_flat, 8, width), f32),
            dma((6,)),
            dma((2,)),
            dma((2 * (n_keys - 1),)),
            dma((2 * (n_keys - 1),)),
            dma((2 * n_flat - 1,)),
            dma((2 * n_flat - 1,)),
            dma((2 * n_flat,)),
            dma((2 * n_flat,)),
            dma((2 * n_flat,)),
            dma((2 * n_flat,)),
            dma((n_flat,)),
            dma((n_flat,)),
        ],
        compiler_params=pltpu.CompilerParams(
            collective_id=0, has_side_effects=True, vmem_limit_bytes=63 * 2**20
        ),
        cost_estimate=pl.CostEstimate(
            flops=flops, bytes_accessed=4 * rows * width, transcendentals=rows * n_slots
        ),
    )(
        entry, visits, doc_length, queries.reshape(rows, width), cache_keys, cache_values,
        slot_params, first_moment, second_moment,
    )
    out = pl.pallas_call(
        write_kernel,
        out_shape=(jax.ShapeDtypeStruct((rows, width), bf16), owned, owned, owned, owned),
        in_specs=[hbm, hbm],
        out_specs=(hbm,) * 5,
        scratch_shapes=[dma((5,))],
        compiler_params=pltpu.CompilerParams(vmem_limit_bytes=63 * 2**20),
    )(teach, stacked)
    return (out[0].reshape(tok, heads, width),) + tuple(out[1:]) + (loss,)


def body(*args):
    per = args[6].shape[0]
    if per % 16 == 0 and lax.axis_size("keys") % 2 == 0:
        return fused(*args)
    return ringed(*args)


def solution(mesh):
    return jax.shard_map(
        body,
        mesh=mesh,
        in_specs=(
            P(("grp", "keys", "qry"), None, None),
            P(("grp", "keys"), None),
            P(("grp", "keys"), None),
            P(("grp", "keys"), "qry"),
            P(("grp", "keys"), "qry"),
            P("grp"),
            P(("grp", "keys", "qry"), None),
            P(("grp", "keys", "qry"), None),
            P(("grp", "keys", "qry"), None),
        ),
        out_specs=(
            P(("grp", "keys", "qry"), None, None),
            P(("grp", "keys", "qry"), None),
            P(("grp", "keys", "qry"), None),
            P(("grp", "keys", "qry"), None),
            P(("grp", "keys", "qry"), None),
            P("grp"),
        ),
        check_vma=False,
    )
```

```python
import functools
import math

import jax
import jax.numpy as jnp
from jax import lax
from jax.experimental import pallas as pl
from jax.experimental.pallas import tpu as pltpu
from jax.sharding import PartitionSpec as P

NEG = -1e30


def shifted(block, axis, distance):
    devices = range(lax.axis_size(axis))
    route = [((i - distance) % len(devices), i) for i in devices]
    return lax.ppermute(block, axis, route)


def row_scores(left, right):
    return lax.dot_general(
        left, right, (((1,), (1,)), ((), ())), preferred_element_type=jnp.float32
    )


def attend(state, query_blocks, keys, values, shard, length, score_scale):
    block_width = keys.shape[0]
    place = shard * block_width + lax.iota(jnp.int32, block_width)
    live = (place < length)[None, :]

    def one(block_entry):
        query_portion, big, total, acc = block_entry
        logit_score = jnp.where(live, row_scores(query_portion, keys) * score_scale, NEG)
        new_big = jnp.maximum(big, jnp.max(logit_score, axis=1))
        weight = jnp.where(live, jnp.exp(logit_score - new_big[:, None]), 0.0)
        fade = jnp.exp(big - new_big)
        total = total * fade + jnp.sum(weight, axis=1)
        acc = acc * fade[:, None] + jnp.dot(
            weight.astype(jnp.bfloat16), values, preferred_element_type=jnp.float32
        )
        return (new_big, total, acc)

    big, total, acc = state
    return lax.map(one, (query_blocks, big, total, acc))


def student_tile(loop_state, block_entry, student_keys, student_values, score_scale):
    key_gradient, squared_terms = loop_state
    query_portion, target = block_entry
    logit_score = row_scores(query_portion, student_keys) * score_scale
    peak = jnp.max(logit_score, axis=1, keepdims=True)
    weight = jnp.exp(logit_score - peak)
    prob = weight / jnp.sum(weight, axis=1, keepdims=True)
    block_prob = prob.astype(jnp.bfloat16)
    student_output = jnp.dot(block_prob, student_values, preferred_element_type=jnp.float32)
    diff = student_output - target.astype(jnp.float32)
    squared_terms = squared_terms + jnp.sum(diff * diff)
    block_difference = diff.astype(jnp.bfloat16)
    prob_gradient = row_scores(block_difference, student_values)
    inner = jnp.sum(prob * prob_gradient, axis=1, keepdims=True)
    dscore = (prob * (prob_gradient - inner) * score_scale).astype(jnp.bfloat16)
    dkeys = lax.dot_general(
        dscore, query_portion, (((0,), (0,)), ((), ())), preferred_element_type=jnp.float32
    )
    dvals = lax.dot_general(
        block_prob, block_difference, (((0,), (0,)), ((), ())), preferred_element_type=jnp.float32
    )
    key_gradient = key_gradient + jnp.concatenate([dkeys, dvals], axis=1)
    return ((key_gradient, squared_terms), None)


def ringed(
    queries,
    cache_keys,
    cache_values,
    entry,
    visits,
    doc_length,
    slot_params,
    first_moment,
    second_moment,
):
    shards = lax.axis_size("keys")
    me = lax.axis_index("keys")
    tok, heads, block_width = queries.shape
    rows = tok * heads
    block = math.gcd(rows, 512)
    nblocks = rows // block
    score_scale = 1.0 / math.sqrt(block_width)
    length = doc_length[0]
    query_blocks = queries.reshape(nblocks, block, block_width)
    start = entry[0, 0]
    count = visits[0, 0]
    state = (
        jnp.full((nblocks, block), NEG, jnp.float32),
        jnp.zeros((nblocks, block), jnp.float32),
        jnp.zeros((nblocks, block, block_width), jnp.float32),
    )

    def visit(step, keys, values, loop_state):
        held = jnp.remainder(me - step, shards)
        go = jnp.remainder(-step - start, shards) < count
        return lax.cond(
            go,
            lambda column_index: attend(
                column_index, query_blocks, keys, values, held, length, score_scale
            ),
            lambda column_index: column_index,
            loop_state,
        )

    def turn(step, loop_state):
        keys, values, big, total, acc = loop_state
        big, total, acc = visit(step, keys, values, (big, total, acc))
        keys, values = shifted((keys, values), "keys", 1)
        return (keys, values, big, total, acc)

    keys, values, big, total, acc = lax.fori_loop(
        0, shards - 1, turn, (cache_keys, cache_values) + state
    )
    big, total, acc = visit(shards - 1, keys, values, (big, total, acc))
    teacher_block_list = (acc / total[:, :, None]).astype(jnp.bfloat16)
    teacher_out = teacher_block_list.reshape(tok, heads, block_width)
    copies = slot_params.astype(jnp.bfloat16)
    complete_sum = lax.all_gather(copies, ("keys", "qry"), axis=0, tiled=True)
    student_keys = complete_sum[:, :block_width]
    student_values = complete_sum[:, block_width:]
    initial_state = (jnp.zeros(complete_sum.shape, jnp.float32), jnp.zeros((), jnp.float32))
    (grad_terms, squared_terms), ignored_value = lax.scan(
        lambda column_index, loop_index: student_tile(
            column_index, loop_index, student_keys, student_values, score_scale
        ),
        initial_state,
        (query_blocks, teacher_block_list),
    )
    slot_grad = lax.psum_scatter(grad_terms, ("keys", "qry"), scatter_dimension=0, tiled=True)
    squares_all = lax.psum(squared_terms, ("keys", "qry"))
    loss = (squares_all / (rows * shards * lax.axis_size("qry"))).reshape(1)
    new_first = 0.9 * first_moment + 0.1 * slot_grad
    new_second = 0.95 * second_moment + 0.05 * slot_grad * slot_grad
    new_params = slot_params - 0.02 * new_first / (jnp.sqrt(new_second) + 1e-08)
    return (teacher_out, slot_grad, new_params, new_first, new_second, loss)


MESH = pl.DeviceIdType.MESH
LOW = -1e20
LOG2E = 1.4426950408889634


def pair_dot(left, right):
    return lax.dot_general(
        left, right, (((1,), (0,)), ((), ())), preferred_element_type=jnp.float32
    )


def step_kernel(
    n_keys,
    n_qry,
    entry_ref,
    visits_ref,
    length_ref,
    q_hbm,
    k_hbm,
    v_hbm,
    slot_hbm,
    first_hbm,
    second_hbm,
    teach_hbm,
    owned_hbm,
    loss_ref,
    teach_ref,
    owned_ref,
    q_ref,
    k_ref,
    v_ref,
    slot_ref,
    first_ref,
    second_ref,
    kbuf,
    vbuf,
    slots,
    top,
    acc,
    e_ref,
    pb_ref,
    ds_ref,
    student,
    diffb,
    gmine,
    gsib_out,
    gsib_in,
    gout,
    gin,
    zout,
    zin,
    sq_own,
    sq_sib,
    sq_chip,
    sq_row,
    sq_in,
    in_sem,
    out_sem,
    kv_send,
    kv_recv,
    sl_send,
    sl_recv,
    gs_send,
    gs_recv,
    g_send,
    g_recv,
    z_send,
    z_recv,
    sq_send,
    sq_recv,
):
    n_x = n_keys // 2
    n_flat = n_x * n_qry
    grp = lax.axis_index("grp")
    me_k = lax.axis_index("keys")
    me_q = lax.axis_index("qry")
    x = lax.div(me_k, 2)
    core = lax.rem(me_k, 2)
    sibling = (grp, x * 2 + 1 - core, me_q)
    rows, width = q_ref.shape
    shard_len = k_ref.shape[0]
    per = slot_ref.shape[0]
    n_slots = slots.shape[0] * per
    scale = 1.0 / math.sqrt(width)
    rate = scale * LOG2E
    tile = math.gcd(rows, 256)
    tiles = rows // tile

    def place(at_x, c, at_q):
        return (at_x * 2 + c) * n_qry + at_q

    def on_x(o):
        return lax.rem(x + o + n_x, n_x)

    def on_q(o):
        return lax.rem(me_q + o + n_qry, n_qry)

    def x_peer(o):
        return (grp, on_x(o) * 2 + core, me_q)

    def q_peer(o):
        return (grp, me_k, on_q(o))

    pending = []

    def send(src, dst, ssem, rsem, dev):
        copy = pltpu.make_async_remote_copy(
            src_ref=src, dst_ref=dst, send_sem=ssem, recv_sem=rsem,
            device_id=dev, device_id_type=MESH,
        )
        copy.start()
        pending.append(copy)

    def arrived(ref, ssem, rsem):
        pltpu.make_async_remote_copy(
            src_ref=ref, dst_ref=ref, send_sem=ssem, recv_sem=rsem,
            device_id=sibling, device_id_type=MESH,
        ).wait_recv()

    loads = [
        pltpu.make_async_copy(src, dst, in_sem.at[i])
        for i, (src, dst) in enumerate((
            (slot_hbm, slot_ref), (q_hbm, q_ref), (k_hbm, k_ref), (v_hbm, v_ref),
            (first_hbm, first_ref), (second_hbm, second_ref),
        ))
    ]
    for load in loads:
        load.start()

    barrier = pltpu.get_barrier_semaphore()
    pl.semaphore_signal(barrier, inc=1, device_id=sibling, device_id_type=MESH)
    for o in range(1, n_x):
        pl.semaphore_signal(barrier, inc=1, device_id=x_peer(o), device_id_type=MESH)
    for o in range(1, n_qry):
        pl.semaphore_signal(barrier, inc=1, device_id=q_peer(o), device_id_type=MESH)
    mine = place(x, core, me_q)
    loads[0].wait()
    slots[mine] = slot_ref[...].astype(jnp.bfloat16)
    pl.semaphore_wait(barrier, n_x + n_qry - 1)

    def pass_on(i, block, dev):
        send(slots.at[block], slots.at[block], sl_send.at[i], sl_recv.at[i], dev)

    for o in range(1, n_x):
        pass_on(o * n_qry, mine, x_peer(o))
    for o in range(1, n_qry):
        pass_on(o, mine, q_peer(o))
    pass_on(n_flat, mine, sibling)
    send(k_hbm, kbuf.at[0], kv_send.at[0], kv_recv.at[0], sibling)
    send(v_hbm, vbuf.at[0], kv_send.at[1], kv_recv.at[1], sibling)
    for j in range(1, n_x):
        there = (grp, lax.rem(x + j, n_x) * 2 + core, me_q)
        s = 2 * j - 1
        send(k_hbm, kbuf.at[s], kv_send.at[2 * s], kv_recv.at[2 * s], there)
        send(v_hbm, vbuf.at[s], kv_send.at[2 * s + 1], kv_recv.at[2 * s + 1], there)

    start = entry_ref[0, 0]
    count = visits_ref[0, 0]
    length = length_ref[0]
    ones = jnp.ones((shard_len, width), jnp.bfloat16)

    def attend(keys_ref, values_ref, shard, is_first):
        col = lax.broadcasted_iota(jnp.int32, (1, shard_len), 1) + shard * shard_len
        turn = lax.rem(shard - me_k - start + 2 * n_keys, n_keys)
        limit = jnp.where(turn < count, length, 0)
        bias = jnp.where(col < limit, 0.0, NEG)

        def one(t, carry):
            at = pl.ds(pl.multiple_of(t * tile, tile), tile)
            score = row_scores(q_ref[at, :], keys_ref[...]) + bias
            peak = jnp.max(score, axis=1, keepdims=True)
            values = jnp.concatenate([values_ref[...], ones], axis=1)
            if is_first:
                new = jnp.maximum(peak, LOW)
                weight = jnp.exp2((score - new) * rate)
                acc[at, :] = pair_dot(weight.astype(jnp.bfloat16), values)
            else:
                old = top[at, 0:1]
                new = jnp.maximum(peak, old)
                weight = jnp.exp2((score - new) * rate)
                fade = jnp.exp2((old - new) * rate)
                acc[at, :] = acc[at, :] * fade + pair_dot(weight.astype(jnp.bfloat16), values)
            top[at, :] = jnp.broadcast_to(new, (tile, width))
            return carry

        lax.fori_loop(0, tiles, one, 0, unroll=2)

    for load in loads[1:4]:
        load.wait()
    attend(k_ref, v_ref, me_k, True)
    for o in range(1, n_x):
        block = place(on_x(-o), core, me_q)
        arrived(slots.at[block], sl_send.at[o * n_qry], sl_recv.at[o * n_qry])
        for z in range(1, n_qry):
            pass_on(o * n_qry + z, block, q_peer(z))
        pass_on(n_flat + o * n_qry, block, sibling)
    arrived(kbuf.at[0], kv_send.at[0], kv_recv.at[0])
    arrived(vbuf.at[0], kv_send.at[1], kv_recv.at[1])
    attend(kbuf.at[0], vbuf.at[0], x * 2 + 1 - core, False)
    for o in range(n_x):
        for z in range(1, n_qry):
            i = o * n_qry + z
            block = place(on_x(-o), core, on_q(-z))
            arrived(slots.at[block], sl_send.at[i], sl_recv.at[i])
            pass_on(n_flat + i, block, sibling)
    for o in range(n_x):
        for z in range(n_qry):
            i = n_flat + o * n_qry + z
            arrived(slots.at[place(on_x(-o), 1 - core, on_q(-z))], sl_send.at[i], sl_recv.at[i])

    def slot_keys():
        return slots[:, :, 0:width].reshape(n_slots, width)

    def slot_values():
        return slots[:, :, width:].reshape(n_slots, width)

    def grouped(value):
        return value.reshape(slots.shape[0], per, tile)

    values_t = slot_values().astype(jnp.float32).T.astype(jnp.bfloat16)

    def softmax(t, carry):
        at = pl.ds(pl.multiple_of(t * tile, tile), tile)
        score = row_scores(slot_keys(), q_ref[at, :])
        peak = jnp.max(score, axis=0, keepdims=True)
        weight = jnp.exp2((score - peak) * rate)
        prob = weight * (1.0 / jnp.sum(weight, axis=0, keepdims=True))
        e_ref[:, :, at] = grouped(prob)
        prob_b = prob.astype(jnp.bfloat16)
        pb_ref[:, :, at] = grouped(prob_b)
        student[at, :] = pair_dot(values_t, prob_b).T
        return carry

    lax.fori_loop(0, tiles, softmax, 0)

    for j in range(1, n_x):
        s = 2 * j - 1
        arrived(kbuf.at[s], kv_send.at[2 * s], kv_recv.at[2 * s])
        arrived(vbuf.at[s], kv_send.at[2 * s + 1], kv_recv.at[2 * s + 1])
        g = s + 1
        send(kbuf.at[s], kbuf.at[g], kv_send.at[2 * g], kv_recv.at[2 * g], sibling)
        send(vbuf.at[s], vbuf.at[g], kv_send.at[2 * g + 1], kv_recv.at[2 * g + 1], sibling)
    for j in range(1, n_x):
        far = lax.rem(x + n_x - j, n_x) * 2
        s = 2 * j - 1
        attend(kbuf.at[s], vbuf.at[s], far + core, False)
        g = s + 1
        arrived(kbuf.at[g], kv_send.at[2 * g], kv_recv.at[2 * g])
        arrived(vbuf.at[g], kv_send.at[2 * g + 1], kv_recv.at[2 * g + 1])
        attend(kbuf.at[g], vbuf.at[g], far + 1 - core, False)

    sq_own[...] = jnp.zeros_like(sq_own)
    for t in range(tiles):
        at = pl.ds(t * tile, tile)
        teacher = (acc[at, 0:width] / acc[at, width:]).astype(jnp.bfloat16)
        teach_ref[at, :] = teacher
        diff = student[at, :] - teacher.astype(jnp.float32)
        sq_own[...] += jnp.sum((diff * diff).reshape(tile // 8, 8, width), axis=0)
        diffb[at, :] = diff.astype(jnp.bfloat16)
    write_teach = pltpu.make_async_copy(teach_ref, teach_hbm, out_sem.at[0])
    write_teach.start()
    send(sq_own, sq_sib, sq_send.at[0], sq_recv.at[0], sibling)

    VALUES, KEYS = 0, 1

    def produce(half):
        left, right = ((pb_ref, diffb), (ds_ref, q_ref))[half]
        for o in list(range(1, n_x)) + [0]:
            for c, to in ((1 - core, gsib_out), (core, gmine)):
                block = left[pl.ds(place(on_x(o), c, 0), n_qry)].reshape(n_qry * per, rows)
                to[half, o] = pair_dot(block, right[...]).reshape(n_qry, per, width)
                if to is gsib_out:
                    sem = half * n_x + o
                    send(gsib_out.at[half, o], gsib_in.at[half, o], gs_send.at[sem], gs_recv.at[sem], sibling)

    def to_x(half):
        for o in range(1, n_x):
            sem = half * n_x + o
            arrived(gsib_in.at[half, o], gs_send.at[sem], gs_recv.at[sem])
            gout[half, o] = (gmine[half, o] + gsib_in[half, o]).astype(jnp.bfloat16)
            send(gout.at[half, o], gin.at[half, o], g_send.at[sem], g_recv.at[sem], x_peer(o))

    def to_z(half):
        arrived(gsib_in.at[half, 0], gs_send.at[half * n_x], gs_recv.at[half * n_x])
        total = gmine[half, 0] + gsib_in[half, 0]
        for o in range(1, n_x):
            sem = half * n_x + o
            arrived(gin.at[half, o], g_send.at[sem], g_recv.at[sem])
            total = total + gin[half, o].astype(jnp.float32)
        gmine[half, 0] = total
        zout[half] = total.astype(jnp.bfloat16)
        for o in range(1, n_qry):
            sem = half * n_qry + o
            send(zout.at[half, on_q(o)], zin.at[half, o], z_send.at[sem], z_recv.at[sem], q_peer(o))

    produce(VALUES)
    to_x(VALUES)
    arrived(sq_sib, sq_send.at[0], sq_recv.at[0])
    sq_chip[...] = sq_own[...] + sq_sib[...]
    for o in range(1, n_x):
        send(sq_chip, sq_in.at[o], sq_send.at[o], sq_recv.at[o], x_peer(o))

    for t in range(tiles):
        at = pl.ds(t * tile, tile)
        dprob = row_scores(slot_values(), diffb[at, :])
        prob = e_ref[:, :, at].reshape(n_slots, tile)
        inner = jnp.sum(prob * dprob, axis=0, keepdims=True)
        ds_ref[:, :, at] = grouped((prob * (dprob - inner) * scale).astype(jnp.bfloat16))
        if t == tiles // 2:
            to_z(VALUES)

    produce(KEYS)
    to_x(KEYS)
    squares = sq_chip[...]
    for o in range(1, n_x):
        arrived(sq_in.at[o], sq_send.at[o], sq_recv.at[o])
        squares = squares + sq_in[o]
    sq_row[...] = squares
    for o in range(1, n_qry):
        i = n_x - 1 + o
        send(sq_row, sq_in.at[i], sq_send.at[i], sq_recv.at[i], q_peer(o))
    to_z(KEYS)
    for o in range(1, n_qry):
        i = n_x - 1 + o
        arrived(sq_in.at[i], sq_send.at[i], sq_recv.at[i])
        squares = squares + sq_in[i]
    loss_ref[0] = jnp.sum(squares) * (1.0 / (rows * n_keys * n_qry))
    for load in loads[4:]:
        load.wait()
    for half in (VALUES, KEYS):
        total = gmine[half, 0, me_q]
        for o in range(1, n_qry):
            i = half * n_qry + o
            arrived(zin.at[half, o], z_send.at[i], z_recv.at[i])
            total = total + zin[half, o].astype(jnp.float32)
        part = pl.ds(width if half == VALUES else 0, width)
        new_first = 0.9 * first_ref[:, part] + 0.1 * total
        new_second = 0.95 * second_ref[:, part] + 0.05 * total * total
        owned_ref[0, :, part] = total
        owned_ref[1, :, part] = slot_ref[:, part] - 0.02 * new_first / (jnp.sqrt(new_second) + 1e-08)
        owned_ref[2, :, part] = new_first
        owned_ref[3, :, part] = new_second
    write_owned = pltpu.make_async_copy(owned_ref, owned_hbm, out_sem.at[1])
    write_owned.start()
    write_teach.wait()
    write_owned.wait()
    for copy in pending:
        copy.wait_send()


def write_kernel(teach_hbm, owned_hbm, teach_out, grad_out, params_out, first_out, second_out, teach, owned, sems):
    load_owned = pltpu.make_async_copy(owned_hbm, owned, sems.at[5])
    load_teach = pltpu.make_async_copy(teach_hbm, teach, sems.at[6])
    load_owned.start()
    load_teach.start()
    load_owned.wait()
    copies = [
        pltpu.make_async_copy(owned.at[i], out, sems.at[i])
        for i, out in enumerate((grad_out, params_out, first_out, second_out))
    ]
    for copy in copies:
        copy.start()
    load_teach.wait()
    copies.append(pltpu.make_async_copy(teach, teach_out, sems.at[4]))
    copies[4].start()
    for copy in copies:
        copy.wait()


def fused(
    queries, cache_keys, cache_values, entry, visits, doc_length, slot_params,
    first_moment, second_moment,
):
    n_keys = lax.axis_size("keys")
    n_qry = lax.axis_size("qry")
    n_x = n_keys // 2
    n_flat = n_x * n_qry
    n_blocks = n_keys * n_qry
    tok, heads, width = queries.shape
    rows = tok * heads
    per, wide = slot_params.shape
    shard_len = cache_keys.shape[0]
    n_slots = per * n_blocks
    f32, bf16 = jnp.float32, jnp.bfloat16
    hbm = pl.BlockSpec(memory_space=pltpu.HBM)
    smem = pl.BlockSpec(memory_space=pltpu.SMEM)
    dma = pltpu.SemaphoreType.DMA
    owned = jax.ShapeDtypeStruct((per, wide), f32)
    flops = 2 * rows * width * (2 * n_keys * shard_len + 5 * n_slots)
    teach, stacked, loss = pl.pallas_call(
        functools.partial(step_kernel, n_keys, n_qry),
        out_shape=(
            jax.ShapeDtypeStruct((rows, width), bf16),
            jax.ShapeDtypeStruct((4, per, wide), f32),
            jax.ShapeDtypeStruct((1,), f32),
        ),
        in_specs=[smem] * 3 + [hbm] * 6,
        out_specs=(hbm, hbm, smem),
        scratch_shapes=[
            pltpu.VMEM((rows, width), bf16),
            pltpu.VMEM((4, per, wide), f32),
            pltpu.VMEM((rows, width), bf16),
            pltpu.VMEM((shard_len, width), bf16),
            pltpu.VMEM((shard_len, width), bf16),
            pltpu.VMEM((per, wide), f32),
            pltpu.VMEM((per, wide), f32),
            pltpu.VMEM((per, wide), f32),
            pltpu.VMEM((n_keys - 1, shard_len, width), bf16),
            pltpu.VMEM((n_keys - 1, shard_len, width), bf16),
            pltpu.VMEM((n_blocks, per, wide), bf16),
            pltpu.VMEM((rows, width), f32),
            pltpu.VMEM((rows, 2 * width), f32),
            pltpu.VMEM((n_blocks, per, rows), f32),
            pltpu.VMEM((n_blocks, per, rows), bf16),
            pltpu.VMEM((n_blocks, per, rows), bf16),
            pltpu.VMEM((rows, width), f32),
            pltpu.VMEM((rows, width), bf16),
            pltpu.VMEM((2, n_x, n_qry, per, width), f32),
            pltpu.VMEM((2, n_x, n_qry, per, width), f32),
            pltpu.VMEM((2, n_x, n_qry, per, width), f32),
            pltpu.VMEM((2, n_x, n_qry, per, width), bf16),
            pltpu.VMEM((2, n_x, n_qry, per, width), bf16),
            pltpu.VMEM((2, n_qry, per, width), bf16),
            pltpu.VMEM((2, n_qry, per, width), bf16),
            pltpu.VMEM((8, width), f32),
            pltpu.VMEM((8, width), f32),
            pltpu.VMEM((8, width), f32),
            pltpu.VMEM((8, width), f32),
            pltpu.VMEM((n_x + n_qry, 8, width), f32),
            dma((6,)),
            dma((2,)),
            dma((2 * (n_keys - 1),)),
            dma((2 * (n_keys - 1),)),
            dma((2 * n_flat,)),
            dma((2 * n_flat,)),
            dma((2 * n_x,)),
            dma((2 * n_x,)),
            dma((2 * n_x,)),
            dma((2 * n_x,)),
            dma((2 * n_qry,)),
            dma((2 * n_qry,)),
            dma((n_x + n_qry,)),
            dma((n_x + n_qry,)),
        ],
        compiler_params=pltpu.CompilerParams(
            collective_id=0, has_side_effects=True, vmem_limit_bytes=63 * 2**20
        ),
        cost_estimate=pl.CostEstimate(
            flops=flops, bytes_accessed=4 * rows * width, transcendentals=rows * n_slots
        ),
    )(
        entry, visits, doc_length, queries.reshape(rows, width), cache_keys, cache_values,
        slot_params, first_moment, second_moment,
    )
    out = pl.pallas_call(
        write_kernel,
        out_shape=(jax.ShapeDtypeStruct((rows, width), bf16), owned, owned, owned, owned),
        in_specs=[hbm, hbm],
        out_specs=(hbm,) * 5,
        scratch_shapes=[pltpu.VMEM((rows, width), bf16), pltpu.VMEM((4, per, wide), f32), dma((7,))],
        compiler_params=pltpu.CompilerParams(vmem_limit_bytes=63 * 2**20),
    )(teach, stacked)
    return (out[0].reshape(tok, heads, width),) + tuple(out[1:]) + (loss,)


def body(*args):
    per = args[6].shape[0]
    if per % 16 == 0 and lax.axis_size("keys") % 2 == 0:
        return fused(*args)
    return ringed(*args)


def solution(mesh):
    return jax.shard_map(
        body,
        mesh=mesh,
        in_specs=(
            P(("grp", "keys", "qry"), None, None),
            P(("grp", "keys"), None),
            P(("grp", "keys"), None),
            P(("grp", "keys"), "qry"),
            P(("grp", "keys"), "qry"),
            P("grp"),
            P(("grp", "keys", "qry"), None),
            P(("grp", "keys", "qry"), None),
            P(("grp", "keys", "qry"), None),
        ),
        out_specs=(
            P(("grp", "keys", "qry"), None, None),
            P(("grp", "keys", "qry"), None),
            P(("grp", "keys", "qry"), None),
            P(("grp", "keys", "qry"), None),
            P(("grp", "keys", "qry"), None),
            P("grp"),
        ),
        check_vma=False,
    )
```

```python
import functools
import math

import jax
import jax.numpy as jnp
from jax import lax
from jax.experimental import pallas as pl
from jax.experimental.pallas import tpu as pltpu
from jax.sharding import PartitionSpec as P

NEG = -1e30


def shifted(block, axis, distance):
    devices = range(lax.axis_size(axis))
    route = [((i - distance) % len(devices), i) for i in devices]
    return lax.ppermute(block, axis, route)


def row_scores(left, right):
    return lax.dot_general(
        left, right, (((1,), (1,)), ((), ())), preferred_element_type=jnp.float32
    )


def attend(state, query_blocks, keys, values, shard, length, score_scale):
    block_width = keys.shape[0]
    place = shard * block_width + lax.iota(jnp.int32, block_width)
    live = (place < length)[None, :]

    def one(block_entry):
        query_portion, big, total, acc = block_entry
        logit_score = jnp.where(live, row_scores(query_portion, keys) * score_scale, NEG)
        new_big = jnp.maximum(big, jnp.max(logit_score, axis=1))
        weight = jnp.where(live, jnp.exp(logit_score - new_big[:, None]), 0.0)
        fade = jnp.exp(big - new_big)
        total = total * fade + jnp.sum(weight, axis=1)
        acc = acc * fade[:, None] + jnp.dot(
            weight.astype(jnp.bfloat16), values, preferred_element_type=jnp.float32
        )
        return (new_big, total, acc)

    big, total, acc = state
    return lax.map(one, (query_blocks, big, total, acc))


def student_tile(loop_state, block_entry, student_keys, student_values, score_scale):
    key_gradient, squared_terms = loop_state
    query_portion, target = block_entry
    logit_score = row_scores(query_portion, student_keys) * score_scale
    peak = jnp.max(logit_score, axis=1, keepdims=True)
    weight = jnp.exp(logit_score - peak)
    prob = weight / jnp.sum(weight, axis=1, keepdims=True)
    block_prob = prob.astype(jnp.bfloat16)
    student_output = jnp.dot(block_prob, student_values, preferred_element_type=jnp.float32)
    diff = student_output - target.astype(jnp.float32)
    squared_terms = squared_terms + jnp.sum(diff * diff)
    block_difference = diff.astype(jnp.bfloat16)
    prob_gradient = row_scores(block_difference, student_values)
    inner = jnp.sum(prob * prob_gradient, axis=1, keepdims=True)
    dscore = (prob * (prob_gradient - inner) * score_scale).astype(jnp.bfloat16)
    dkeys = lax.dot_general(
        dscore, query_portion, (((0,), (0,)), ((), ())), preferred_element_type=jnp.float32
    )
    dvals = lax.dot_general(
        block_prob, block_difference, (((0,), (0,)), ((), ())), preferred_element_type=jnp.float32
    )
    key_gradient = key_gradient + jnp.concatenate([dkeys, dvals], axis=1)
    return ((key_gradient, squared_terms), None)


def ringed(
    queries,
    cache_keys,
    cache_values,
    entry,
    visits,
    doc_length,
    slot_params,
    first_moment,
    second_moment,
):
    shards = lax.axis_size("keys")
    me = lax.axis_index("keys")
    tok, heads, block_width = queries.shape
    rows = tok * heads
    block = math.gcd(rows, 512)
    nblocks = rows // block
    score_scale = 1.0 / math.sqrt(block_width)
    length = doc_length[0]
    query_blocks = queries.reshape(nblocks, block, block_width)
    start = entry[0, 0]
    count = visits[0, 0]
    state = (
        jnp.full((nblocks, block), NEG, jnp.float32),
        jnp.zeros((nblocks, block), jnp.float32),
        jnp.zeros((nblocks, block, block_width), jnp.float32),
    )

    def visit(step, keys, values, loop_state):
        held = jnp.remainder(me - step, shards)
        go = jnp.remainder(-step - start, shards) < count
        return lax.cond(
            go,
            lambda column_index: attend(
                column_index, query_blocks, keys, values, held, length, score_scale
            ),
            lambda column_index: column_index,
            loop_state,
        )

    def turn(step, loop_state):
        keys, values, big, total, acc = loop_state
        big, total, acc = visit(step, keys, values, (big, total, acc))
        keys, values = shifted((keys, values), "keys", 1)
        return (keys, values, big, total, acc)

    keys, values, big, total, acc = lax.fori_loop(
        0, shards - 1, turn, (cache_keys, cache_values) + state
    )
    big, total, acc = visit(shards - 1, keys, values, (big, total, acc))
    teacher_block_list = (acc / total[:, :, None]).astype(jnp.bfloat16)
    teacher_out = teacher_block_list.reshape(tok, heads, block_width)
    copies = slot_params.astype(jnp.bfloat16)
    complete_sum = lax.all_gather(copies, ("keys", "qry"), axis=0, tiled=True)
    student_keys = complete_sum[:, :block_width]
    student_values = complete_sum[:, block_width:]
    initial_state = (jnp.zeros(complete_sum.shape, jnp.float32), jnp.zeros((), jnp.float32))
    (grad_terms, squared_terms), ignored_value = lax.scan(
        lambda column_index, loop_index: student_tile(
            column_index, loop_index, student_keys, student_values, score_scale
        ),
        initial_state,
        (query_blocks, teacher_block_list),
    )
    slot_grad = lax.psum_scatter(grad_terms, ("keys", "qry"), scatter_dimension=0, tiled=True)
    squares_all = lax.psum(squared_terms, ("keys", "qry"))
    loss = (squares_all / (rows * shards * lax.axis_size("qry"))).reshape(1)
    new_first = 0.9 * first_moment + 0.1 * slot_grad
    new_second = 0.95 * second_moment + 0.05 * slot_grad * slot_grad
    new_params = slot_params - 0.02 * new_first / (jnp.sqrt(new_second) + 1e-08)
    return (teacher_out, slot_grad, new_params, new_first, new_second, loss)


MESH = pl.DeviceIdType.MESH
LOW = -1e20
LOG2E = 1.4426950408889634


def pair_dot(left, right):
    return lax.dot_general(
        left, right, (((1,), (0,)), ((), ())), preferred_element_type=jnp.float32
    )


def step_kernel(
    n_keys,
    n_qry,
    entry_ref,
    visits_ref,
    length_ref,
    q_hbm,
    k_hbm,
    v_hbm,
    slot_hbm,
    first_hbm,
    second_hbm,
    teach_hbm,
    owned_hbm,
    loss_hbm,
    teach_ref,
    owned_ref,
    loss_ref,
    q_ref,
    k_ref,
    v_ref,
    slot_ref,
    first_ref,
    second_ref,
    kbuf,
    vbuf,
    slots,
    top,
    acc,
    e_ref,
    pb_ref,
    ds_ref,
    student,
    diffb,
    gmine,
    gsib_out,
    gsib_in,
    gout,
    gin,
    sq_own,
    sq_sib,
    sq_chip,
    sq_in,
    in_sem,
    out_sem,
    kv_send,
    kv_recv,
    sl_send,
    sl_recv,
    gs_send,
    gs_recv,
    g_send,
    g_recv,
    sq_send,
    sq_recv,
):
    n_x = n_keys // 2
    n_flat = n_x * n_qry
    grp = lax.axis_index("grp")
    me_k = lax.axis_index("keys")
    me_q = lax.axis_index("qry")
    x = lax.div(me_k, 2)
    core = lax.rem(me_k, 2)
    flat = x * n_qry + me_q
    sibling = (grp, x * 2 + 1 - core, me_q)
    rows, width = q_ref.shape
    shard_len = k_ref.shape[0]
    per = slot_ref.shape[0]
    n_slots = slots.shape[0] * per
    scale = 1.0 / math.sqrt(width)
    rate = scale * LOG2E
    tile = math.gcd(rows, 256)
    tiles = rows // tile

    def place(f, c):
        return (lax.div(f, n_qry) * 2 + c) * n_qry + lax.rem(f, n_qry)

    def peer(f):
        return (grp, lax.div(f, n_qry) * 2 + core, lax.rem(f, n_qry))

    def ahead(o):
        return lax.rem(flat + o, n_flat)

    def behind(o):
        return lax.rem(flat + n_flat - o, n_flat)

    pending = []

    def send(src, dst, ssem, rsem, dev):
        copy = pltpu.make_async_remote_copy(
            src_ref=src, dst_ref=dst, send_sem=ssem, recv_sem=rsem,
            device_id=dev, device_id_type=MESH,
        )
        copy.start()
        pending.append(copy)

    def arrived(ref, ssem, rsem):
        pltpu.make_async_remote_copy(
            src_ref=ref, dst_ref=ref, send_sem=ssem, recv_sem=rsem,
            device_id=sibling, device_id_type=MESH,
        ).wait_recv()

    loads = [
        pltpu.make_async_copy(src, dst, in_sem.at[i])
        for i, (src, dst) in enumerate((
            (slot_hbm, slot_ref), (q_hbm, q_ref), (k_hbm, k_ref), (v_hbm, v_ref),
            (first_hbm, first_ref), (second_hbm, second_ref),
        ))
    ]
    for load in loads:
        load.start()

    barrier = pltpu.get_barrier_semaphore()
    pl.semaphore_signal(barrier, inc=1, device_id=sibling, device_id_type=MESH)
    for o in range(1, n_flat):
        pl.semaphore_signal(barrier, inc=1, device_id=peer(ahead(o)), device_id_type=MESH)
    mine = place(flat, core)
    loads[0].wait()
    slots[mine] = slot_ref[...].astype(jnp.bfloat16)
    pl.semaphore_wait(barrier, n_flat)

    send(slots.at[mine], slots.at[mine], sl_send.at[0], sl_recv.at[0], sibling)
    send(k_hbm, kbuf.at[0], kv_send.at[0], kv_recv.at[0], sibling)
    send(v_hbm, vbuf.at[0], kv_send.at[1], kv_recv.at[1], sibling)
    for o in range(1, n_flat):
        send(slots.at[mine], slots.at[mine], sl_send.at[o], sl_recv.at[o], peer(ahead(o)))
    for j in range(1, n_x):
        there = (grp, lax.rem(x + j, n_x) * 2 + core, me_q)
        s = 2 * j - 1
        send(k_hbm, kbuf.at[s], kv_send.at[2 * s], kv_recv.at[2 * s], there)
        send(v_hbm, vbuf.at[s], kv_send.at[2 * s + 1], kv_recv.at[2 * s + 1], there)

    for load in loads[1:4]:
        load.wait()
    start = entry_ref[0, 0]
    count = visits_ref[0, 0]
    length = length_ref[0]
    ones = jnp.ones((shard_len, width), jnp.bfloat16)

    def attend(keys_ref, values_ref, shard, is_first):
        col = lax.broadcasted_iota(jnp.int32, (1, shard_len), 1) + shard * shard_len
        turn = lax.rem(shard - me_k - start + 2 * n_keys, n_keys)
        limit = jnp.where(turn < count, length, 0)
        bias = jnp.where(col < limit, 0.0, NEG)

        for t in range(tiles):
            at = pl.ds(t * tile, tile)
            score = row_scores(q_ref[at, :], keys_ref[...]) + bias
            peak = jnp.max(score, axis=1, keepdims=True)
            values = jnp.concatenate([values_ref[...], ones], axis=1)
            if is_first:
                new = jnp.maximum(peak, LOW)
                weight = jnp.exp2((score - new) * rate)
                acc[at, :] = pair_dot(weight.astype(jnp.bfloat16), values)
            else:
                old = top[at, 0:1]
                new = jnp.maximum(peak, old)
                weight = jnp.exp2((score - new) * rate)
                fade = jnp.exp2((old - new) * rate)
                acc[at, :] = acc[at, :] * fade + pair_dot(weight.astype(jnp.bfloat16), values)
            top[at, :] = jnp.broadcast_to(new, (tile, width))

    attend(k_ref, v_ref, me_k, True)
    arrived(kbuf.at[0], kv_send.at[0], kv_recv.at[0])
    arrived(vbuf.at[0], kv_send.at[1], kv_recv.at[1])
    attend(kbuf.at[0], vbuf.at[0], x * 2 + 1 - core, False)

    for o in range(1, n_flat):
        block = place(behind(o), core)
        arrived(slots.at[block], sl_send.at[o], sl_recv.at[o])
        i = n_flat - 1 + o
        send(slots.at[block], slots.at[block], sl_send.at[i], sl_recv.at[i], sibling)
    arrived(slots.at[place(flat, 1 - core)], sl_send.at[0], sl_recv.at[0])
    for o in range(1, n_flat):
        i = n_flat - 1 + o
        arrived(slots.at[place(behind(o), 1 - core)], sl_send.at[i], sl_recv.at[i])

    def slot_keys():
        return slots[:, :, 0:width].reshape(n_slots, width)

    def slot_values():
        return slots[:, :, width:].reshape(n_slots, width)

    def grouped(value):
        return value.reshape(slots.shape[0], per, tile)

    values_t = slot_values().astype(jnp.float32).T.astype(jnp.bfloat16)

    for t in range(tiles):
        at = pl.ds(t * tile, tile)
        score = row_scores(slot_keys(), q_ref[at, :])
        peak = jnp.max(score, axis=0, keepdims=True)
        weight = jnp.exp2((score - peak) * rate)
        prob = weight * (1.0 / jnp.sum(weight, axis=0, keepdims=True))
        e_ref[:, :, at] = grouped(prob)
        prob_b = prob.astype(jnp.bfloat16)
        pb_ref[:, :, at] = grouped(prob_b)
        student[at, :] = pair_dot(values_t, prob_b).T

    for j in range(1, n_x):
        s = 2 * j - 1
        arrived(kbuf.at[s], kv_send.at[2 * s], kv_recv.at[2 * s])
        arrived(vbuf.at[s], kv_send.at[2 * s + 1], kv_recv.at[2 * s + 1])
        g = s + 1
        send(kbuf.at[s], kbuf.at[g], kv_send.at[2 * g], kv_recv.at[2 * g], sibling)
        send(vbuf.at[s], vbuf.at[g], kv_send.at[2 * g + 1], kv_recv.at[2 * g + 1], sibling)
    for j in range(1, n_x):
        far = lax.rem(x + n_x - j, n_x) * 2
        s = 2 * j - 1
        attend(kbuf.at[s], vbuf.at[s], far + core, False)
        g = s + 1
        arrived(kbuf.at[g], kv_send.at[2 * g], kv_recv.at[2 * g])
        arrived(vbuf.at[g], kv_send.at[2 * g + 1], kv_recv.at[2 * g + 1])
        attend(kbuf.at[g], vbuf.at[g], far + 1 - core, False)

    sq_own[...] = jnp.zeros_like(sq_own)
    for t in range(tiles):
        at = pl.ds(t * tile, tile)
        teacher = (acc[at, 0:width] / acc[at, width:]).astype(jnp.bfloat16)
        teach_ref[at, :] = teacher
        diff = student[at, :] - teacher.astype(jnp.float32)
        sq_own[...] += jnp.sum((diff * diff).reshape(tile // 8, 8, width), axis=0)
        diffb[at, :] = diff.astype(jnp.bfloat16)
    write_teach = pltpu.make_async_copy(teach_ref, teach_hbm, out_sem.at[0])
    write_teach.start()
    send(sq_own, sq_sib, sq_send.at[0], sq_recv.at[0], sibling)

    order = list(range(1, n_flat)) + [0]
    group = 2 if n_flat % 2 == 0 else 1
    batches = n_flat // group
    VALUES, KEYS = 0, 1

    def produce(half, i):
        left, right = ((pb_ref, diffb), (ds_ref, q_ref))[half]
        first = i * group
        offsets = order[first:first + group]
        blocks = [place(ahead(o), 1 - core) for o in offsets]
        blocks += [place(ahead(o), core) for o in offsets]
        terms = pair_dot(jnp.concatenate([left[b] for b in blocks], axis=0), right[...])
        terms = terms.reshape(2, group, per, width)
        span = pl.ds(first, group)
        gsib_out[half, span] = terms[0]
        gmine[half, span] = terms[1]
        sem = half * batches + i
        send(gsib_out.at[half, span], gsib_in.at[half, span], gs_send.at[sem], gs_recv.at[sem], sibling)

    def finish(half, i):
        first = i * group
        sem = half * batches + i
        arrived(gsib_in.at[half, pl.ds(first, group)], gs_send.at[sem], gs_recv.at[sem])
        for p in range(first, first + group):
            o = order[p]
            if o > 0:
                gout[half, p] = (gmine[half, p] + gsib_in[half, p]).astype(jnp.bfloat16)
                i = half * n_flat + p
                send(gout.at[half, p], gin.at[half, p], g_send.at[i], g_recv.at[i], peer(ahead(o)))

    for i in range(batches):
        produce(VALUES, i)
        if i > 0:
            finish(VALUES, i - 1)
    finish(VALUES, batches - 1)
    arrived(sq_sib, sq_send.at[0], sq_recv.at[0])
    sq_chip[...] = sq_own[...] + sq_sib[...]
    for o in range(1, n_flat):
        send(sq_chip, sq_in.at[o], sq_send.at[o], sq_recv.at[o], peer(ahead(o)))

    for t in range(tiles):
        at = pl.ds(t * tile, tile)
        dprob = row_scores(slot_values(), diffb[at, :])
        prob = e_ref[:, :, at].reshape(n_slots, tile)
        inner = jnp.sum(prob * dprob, axis=0, keepdims=True)
        ds_ref[:, :, at] = grouped((prob * (dprob - inner) * scale).astype(jnp.bfloat16))

    for i in range(batches):
        produce(KEYS, i)
        if i > 0:
            finish(KEYS, i - 1)
    finish(KEYS, batches - 1)

    squares = sq_chip[...]
    for o in range(1, n_flat):
        arrived(sq_in.at[o], sq_send.at[o], sq_recv.at[o])
        squares = squares + sq_in[o]
    loss = jnp.sum(squares, keepdims=True) * (1.0 / (rows * n_keys * n_qry))
    loss_ref[...] = jnp.broadcast_to(loss, loss_ref.shape)
    write_loss = pltpu.make_async_copy(loss_ref, loss_hbm, out_sem.at[2])
    write_loss.start()
    for load in loads[4:]:
        load.wait()
    for half in (VALUES, KEYS):
        total = gmine[half, n_flat - 1] + gsib_in[half, n_flat - 1]
        for p in range(n_flat - 1):
            i = half * n_flat + p
            arrived(gin.at[half, p], g_send.at[i], g_recv.at[i])
            total = total + gin[half, p].astype(jnp.float32)
        part = pl.ds(width if half == VALUES else 0, width)
        new_first = 0.9 * first_ref[:, part] + 0.1 * total
        new_second = 0.95 * second_ref[:, part] + 0.05 * total * total
        owned_ref[0, :, part] = total
        owned_ref[1, :, part] = slot_ref[:, part] - 0.02 * new_first / (jnp.sqrt(new_second) + 1e-08)
        owned_ref[2, :, part] = new_first
        owned_ref[3, :, part] = new_second
    write_owned = pltpu.make_async_copy(owned_ref, owned_hbm, out_sem.at[1])
    write_owned.start()
    write_teach.wait()
    write_owned.wait()
    write_loss.wait()
    for copy in pending:
        copy.wait_send()


def write_kernel(
    teach_hbm, owned_hbm, loss_hbm, teach_out, grad_out, params_out, first_out, second_out, loss_out,
    teach, owned, loss, sems,
):
    loads = [
        pltpu.make_async_copy(src, dst, sems.at[i])
        for i, (src, dst) in enumerate(((owned_hbm, owned), (teach_hbm, teach), (loss_hbm, loss)))
    ]
    for load in loads:
        load.start()
    loads[0].wait()
    copies = [
        pltpu.make_async_copy(owned.at[i], out, sems.at[3 + i])
        for i, out in enumerate((grad_out, params_out, first_out, second_out))
    ]
    for copy in copies:
        copy.start()
    loads[1].wait()
    copies.append(pltpu.make_async_copy(teach, teach_out, sems.at[7]))
    copies[4].start()
    loads[2].wait()
    loss_out[0] = jnp.max(loss[...])
    for copy in copies:
        copy.wait()


def fused(
    queries, cache_keys, cache_values, entry, visits, doc_length, slot_params,
    first_moment, second_moment,
):
    n_keys = lax.axis_size("keys")
    n_qry = lax.axis_size("qry")
    n_flat = n_keys // 2 * n_qry
    n_blocks = n_keys * n_qry
    tok, heads, width = queries.shape
    rows = tok * heads
    per, wide = slot_params.shape
    shard_len = cache_keys.shape[0]
    n_slots = per * n_blocks
    f32, bf16 = jnp.float32, jnp.bfloat16
    hbm = pl.BlockSpec(memory_space=pltpu.HBM)
    smem = pl.BlockSpec(memory_space=pltpu.SMEM)
    dma = pltpu.SemaphoreType.DMA
    owned = jax.ShapeDtypeStruct((per, wide), f32)
    flops = 2 * rows * width * (2 * n_keys * shard_len + 5 * n_slots)
    teach, stacked, loss = pl.pallas_call(
        functools.partial(step_kernel, n_keys, n_qry),
        out_shape=(
            jax.ShapeDtypeStruct((rows, width), bf16),
            jax.ShapeDtypeStruct((4, per, wide), f32),
            jax.ShapeDtypeStruct((8, width), f32),
        ),
        in_specs=[smem] * 3 + [hbm] * 6,
        out_specs=(hbm,) * 3,
        scratch_shapes=[
            pltpu.VMEM((rows, width), bf16),
            pltpu.VMEM((4, per, wide), f32),
            pltpu.VMEM((8, width), f32),
            pltpu.VMEM((rows, width), bf16),
            pltpu.VMEM((shard_len, width), bf16),
            pltpu.VMEM((shard_len, width), bf16),
            pltpu.VMEM((per, wide), f32),
            pltpu.VMEM((per, wide), f32),
            pltpu.VMEM((per, wide), f32),
            pltpu.VMEM((n_keys - 1, shard_len, width), bf16),
            pltpu.VMEM((n_keys - 1, shard_len, width), bf16),
            pltpu.VMEM((n_blocks, per, wide), bf16),
            pltpu.VMEM((rows, width), f32),
            pltpu.VMEM((rows, 2 * width), f32),
            pltpu.VMEM((n_blocks, per, rows), f32),
            pltpu.VMEM((n_blocks, per, rows), bf16),
            pltpu.VMEM((n_blocks, per, rows), bf16),
            pltpu.VMEM((rows, width), f32),
            pltpu.VMEM((rows, width), bf16),
            pltpu.VMEM((2, n_flat, per, width), f32),
            pltpu.VMEM((2, n_flat, per, width), f32),
            pltpu.VMEM((2, n_flat, per, width), f32),
            pltpu.VMEM((2, n_flat, per, width), bf16),
            pltpu.VMEM((2, n_flat, per, width), bf16),
            pltpu.VMEM((8, width), f32),
            pltpu.VMEM((8, width), f32),
            pltpu.VMEM((8, width), f32),
            pltpu.VMEM((n_flat, 8, width), f32),
            dma((6,)),
            dma((3,)),
            dma((2 * (n_keys - 1),)),
            dma((2 * (n_keys - 1),)),
            dma((2 * n_flat - 1,)),
            dma((2 * n_flat - 1,)),
            dma((2 * n_flat,)),
            dma((2 * n_flat,)),
            dma((2 * n_flat,)),
            dma((2 * n_flat,)),
            dma((n_flat,)),
            dma((n_flat,)),
        ],
        compiler_params=pltpu.CompilerParams(
            collective_id=0, has_side_effects=True, vmem_limit_bytes=63 * 2**20
        ),
        cost_estimate=pl.CostEstimate(
            flops=flops, bytes_accessed=4 * rows * width, transcendentals=rows * n_slots
        ),
    )(
        entry, visits, doc_length, queries.reshape(rows, width), cache_keys, cache_values,
        slot_params, first_moment, second_moment,
    )
    out = pl.pallas_call(
        write_kernel,
        out_shape=(
            jax.ShapeDtypeStruct((rows, width), bf16), owned, owned, owned, owned,
            jax.ShapeDtypeStruct((1,), f32),
        ),
        in_specs=[hbm] * 3,
        out_specs=(hbm,) * 5 + (smem,),
        scratch_shapes=[
            pltpu.VMEM((rows, width), bf16),
            pltpu.VMEM((4, per, wide), f32),
            pltpu.VMEM((8, width), f32),
            dma((8,)),
        ],
        compiler_params=pltpu.CompilerParams(vmem_limit_bytes=63 * 2**20),
    )(teach, stacked, loss)
    return (out[0].reshape(tok, heads, width),) + tuple(out[1:])


def body(*args):
    per = args[6].shape[0]
    if per % 16 == 0 and lax.axis_size("keys") % 2 == 0:
        return fused(*args)
    return ringed(*args)


def solution(mesh):
    return jax.shard_map(
        body,
        mesh=mesh,
        in_specs=(
            P(("grp", "keys", "qry"), None, None),
            P(("grp", "keys"), None),
            P(("grp", "keys"), None),
            P(("grp", "keys"), "qry"),
            P(("grp", "keys"), "qry"),
            P("grp"),
            P(("grp", "keys", "qry"), None),
            P(("grp", "keys", "qry"), None),
            P(("grp", "keys", "qry"), None),
        ),
        out_specs=(
            P(("grp", "keys", "qry"), None, None),
            P(("grp", "keys", "qry"), None),
            P(("grp", "keys", "qry"), None),
            P(("grp", "keys", "qry"), None),
            P(("grp", "keys", "qry"), None),
            P("grp"),
        ),
        check_vma=False,
    )
```

```python
import functools
import math

import jax
import jax.numpy as jnp
from jax import lax
from jax.experimental import pallas as pl
from jax.experimental.pallas import tpu as pltpu
from jax.sharding import PartitionSpec as P

NEG = -1e30


def shifted(block, axis, distance):
    devices = range(lax.axis_size(axis))
    route = [((i - distance) % len(devices), i) for i in devices]
    return lax.ppermute(block, axis, route)


def row_scores(left, right):
    return lax.dot_general(
        left, right, (((1,), (1,)), ((), ())), preferred_element_type=jnp.float32
    )


def attend(state, query_blocks, keys, values, shard, length, score_scale):
    block_width = keys.shape[0]
    place = shard * block_width + lax.iota(jnp.int32, block_width)
    live = (place < length)[None, :]

    def one(block_entry):
        query_portion, big, total, acc = block_entry
        logit_score = jnp.where(live, row_scores(query_portion, keys) * score_scale, NEG)
        new_big = jnp.maximum(big, jnp.max(logit_score, axis=1))
        weight = jnp.where(live, jnp.exp(logit_score - new_big[:, None]), 0.0)
        fade = jnp.exp(big - new_big)
        total = total * fade + jnp.sum(weight, axis=1)
        acc = acc * fade[:, None] + jnp.dot(
            weight.astype(jnp.bfloat16), values, preferred_element_type=jnp.float32
        )
        return (new_big, total, acc)

    big, total, acc = state
    return lax.map(one, (query_blocks, big, total, acc))


def student_tile(loop_state, block_entry, student_keys, student_values, score_scale):
    key_gradient, squared_terms = loop_state
    query_portion, target = block_entry
    logit_score = row_scores(query_portion, student_keys) * score_scale
    peak = jnp.max(logit_score, axis=1, keepdims=True)
    weight = jnp.exp(logit_score - peak)
    prob = weight / jnp.sum(weight, axis=1, keepdims=True)
    block_prob = prob.astype(jnp.bfloat16)
    student_output = jnp.dot(block_prob, student_values, preferred_element_type=jnp.float32)
    diff = student_output - target.astype(jnp.float32)
    squared_terms = squared_terms + jnp.sum(diff * diff)
    block_difference = diff.astype(jnp.bfloat16)
    prob_gradient = row_scores(block_difference, student_values)
    inner = jnp.sum(prob * prob_gradient, axis=1, keepdims=True)
    dscore = (prob * (prob_gradient - inner) * score_scale).astype(jnp.bfloat16)
    dkeys = lax.dot_general(
        dscore, query_portion, (((0,), (0,)), ((), ())), preferred_element_type=jnp.float32
    )
    dvals = lax.dot_general(
        block_prob, block_difference, (((0,), (0,)), ((), ())), preferred_element_type=jnp.float32
    )
    key_gradient = key_gradient + jnp.concatenate([dkeys, dvals], axis=1)
    return ((key_gradient, squared_terms), None)


def ringed(
    queries,
    cache_keys,
    cache_values,
    entry,
    visits,
    doc_length,
    slot_params,
    first_moment,
    second_moment,
):
    shards = lax.axis_size("keys")
    me = lax.axis_index("keys")
    tok, heads, block_width = queries.shape
    rows = tok * heads
    block = math.gcd(rows, 512)
    nblocks = rows // block
    score_scale = 1.0 / math.sqrt(block_width)
    length = doc_length[0]
    query_blocks = queries.reshape(nblocks, block, block_width)
    start = entry[0, 0]
    count = visits[0, 0]
    state = (
        jnp.full((nblocks, block), NEG, jnp.float32),
        jnp.zeros((nblocks, block), jnp.float32),
        jnp.zeros((nblocks, block, block_width), jnp.float32),
    )

    def visit(step, keys, values, loop_state):
        held = jnp.remainder(me - step, shards)
        go = jnp.remainder(-step - start, shards) < count
        return lax.cond(
            go,
            lambda column_index: attend(
                column_index, query_blocks, keys, values, held, length, score_scale
            ),
            lambda column_index: column_index,
            loop_state,
        )

    def turn(step, loop_state):
        keys, values, big, total, acc = loop_state
        big, total, acc = visit(step, keys, values, (big, total, acc))
        keys, values = shifted((keys, values), "keys", 1)
        return (keys, values, big, total, acc)

    keys, values, big, total, acc = lax.fori_loop(
        0, shards - 1, turn, (cache_keys, cache_values) + state
    )
    big, total, acc = visit(shards - 1, keys, values, (big, total, acc))
    teacher_block_list = (acc / total[:, :, None]).astype(jnp.bfloat16)
    teacher_out = teacher_block_list.reshape(tok, heads, block_width)
    copies = slot_params.astype(jnp.bfloat16)
    complete_sum = lax.all_gather(copies, ("keys", "qry"), axis=0, tiled=True)
    student_keys = complete_sum[:, :block_width]
    student_values = complete_sum[:, block_width:]
    initial_state = (jnp.zeros(complete_sum.shape, jnp.float32), jnp.zeros((), jnp.float32))
    (grad_terms, squared_terms), ignored_value = lax.scan(
        lambda column_index, loop_index: student_tile(
            column_index, loop_index, student_keys, student_values, score_scale
        ),
        initial_state,
        (query_blocks, teacher_block_list),
    )
    slot_grad = lax.psum_scatter(grad_terms, ("keys", "qry"), scatter_dimension=0, tiled=True)
    squares_all = lax.psum(squared_terms, ("keys", "qry"))
    loss = (squares_all / (rows * shards * lax.axis_size("qry"))).reshape(1)
    new_first = 0.9 * first_moment + 0.1 * slot_grad
    new_second = 0.95 * second_moment + 0.05 * slot_grad * slot_grad
    new_params = slot_params - 0.02 * new_first / (jnp.sqrt(new_second) + 1e-08)
    return (teacher_out, slot_grad, new_params, new_first, new_second, loss)


MESH = pl.DeviceIdType.MESH
LOW = -1e20
LOG2E = 1.4426950408889634


def pair_dot(left, right):
    return lax.dot_general(
        left, right, (((1,), (0,)), ((), ())), preferred_element_type=jnp.float32
    )


def step_kernel(
    n_keys,
    n_qry,
    entry_ref,
    visits_ref,
    length_ref,
    q_hbm,
    k_hbm,
    v_hbm,
    slot_hbm,
    first_hbm,
    second_hbm,
    teach_hbm,
    owned_hbm,
    loss_hbm,
    teach_ref,
    owned_ref,
    loss_ref,
    q_ref,
    k_ref,
    v_ref,
    slot_ref,
    first_ref,
    second_ref,
    kbuf,
    vbuf,
    slots,
    top,
    acc,
    e_ref,
    pb_ref,
    ds_ref,
    student,
    diffb,
    gmine,
    gsib_out,
    gsib_in,
    gout,
    gin,
    sq_own,
    sq_sib,
    sq_chip,
    sq_in,
    in_sem,
    out_sem,
    kv_send,
    kv_recv,
    sl_send,
    sl_recv,
    gs_send,
    gs_recv,
    g_send,
    g_recv,
    sq_send,
    sq_recv,
):
    n_x = n_keys // 2
    n_flat = n_x * n_qry
    grp = lax.axis_index("grp")
    me_k = lax.axis_index("keys")
    me_q = lax.axis_index("qry")
    x = lax.div(me_k, 2)
    core = lax.rem(me_k, 2)
    flat = x * n_qry + me_q
    sibling = (grp, x * 2 + 1 - core, me_q)
    rows, width = q_ref.shape
    shard_len = k_ref.shape[0]
    per = slot_ref.shape[0]
    n_slots = slots.shape[0] * per
    scale = 1.0 / math.sqrt(width)
    rate = scale * LOG2E
    tile = math.gcd(rows, 256)
    tiles = rows // tile

    def place(f, c):
        return (lax.div(f, n_qry) * 2 + c) * n_qry + lax.rem(f, n_qry)

    def peer(f):
        return (grp, lax.div(f, n_qry) * 2 + core, lax.rem(f, n_qry))

    def ahead(o):
        return lax.rem(flat + o, n_flat)

    def behind(o):
        return lax.rem(flat + n_flat - o, n_flat)

    pending = []

    def send(src, dst, ssem, rsem, dev):
        copy = pltpu.make_async_remote_copy(
            src_ref=src, dst_ref=dst, send_sem=ssem, recv_sem=rsem,
            device_id=dev, device_id_type=MESH,
        )
        copy.start()
        pending.append(copy)

    def arrived(ref, ssem, rsem):
        pltpu.make_async_remote_copy(
            src_ref=ref, dst_ref=ref, send_sem=ssem, recv_sem=rsem,
            device_id=sibling, device_id_type=MESH,
        ).wait_recv()

    loads = [
        pltpu.make_async_copy(src, dst, in_sem.at[i])
        for i, (src, dst) in enumerate((
            (slot_hbm, slot_ref), (q_hbm, q_ref), (k_hbm, k_ref), (v_hbm, v_ref),
            (first_hbm, first_ref), (second_hbm, second_ref),
        ))
    ]
    for load in loads:
        load.start()

    barrier = pltpu.get_barrier_semaphore()
    pl.semaphore_signal(barrier, inc=1, device_id=sibling, device_id_type=MESH)
    for o in range(1, n_flat):
        pl.semaphore_signal(barrier, inc=1, device_id=peer(ahead(o)), device_id_type=MESH)
    mine = place(flat, core)
    loads[0].wait()
    slots[mine] = slot_ref[...].astype(jnp.bfloat16)
    pl.semaphore_wait(barrier, n_flat)

    send(slots.at[mine], slots.at[mine], sl_send.at[0], sl_recv.at[0], sibling)
    send(k_hbm, kbuf.at[0], kv_send.at[0], kv_recv.at[0], sibling)
    send(v_hbm, vbuf.at[0], kv_send.at[1], kv_recv.at[1], sibling)
    for o in range(1, n_flat):
        send(slots.at[mine], slots.at[mine], sl_send.at[o], sl_recv.at[o], peer(ahead(o)))
    for j in range(1, n_x):
        there = (grp, lax.rem(x + j, n_x) * 2 + core, me_q)
        s = 2 * j - 1
        send(k_hbm, kbuf.at[s], kv_send.at[2 * s], kv_recv.at[2 * s], there)
        send(v_hbm, vbuf.at[s], kv_send.at[2 * s + 1], kv_recv.at[2 * s + 1], there)

    for load in loads[1:4]:
        load.wait()
    start = entry_ref[0, 0]
    count = visits_ref[0, 0]
    length = length_ref[0]
    ones = jnp.ones((shard_len, width), jnp.bfloat16)

    def attend(keys_ref, values_ref, shard, is_first):
        col = lax.broadcasted_iota(jnp.int32, (1, shard_len), 1) + shard * shard_len
        turn = lax.rem(shard - me_k - start + 2 * n_keys, n_keys)
        limit = jnp.where(turn < count, length, 0)
        bias = jnp.where(col < limit, 0.0, NEG)

        for t in range(tiles):
            at = pl.ds(t * tile, tile)
            score = row_scores(q_ref[at, :], keys_ref[...]) + bias
            peak = jnp.max(score, axis=1, keepdims=True)
            values = jnp.concatenate([values_ref[...], ones], axis=1)
            if is_first:
                new = jnp.maximum(peak, LOW)
                weight = jnp.exp2((score - new) * rate)
                acc[at, :] = pair_dot(weight.astype(jnp.bfloat16), values)
            else:
                old = top[at, 0:1]
                new = jnp.maximum(peak, old)
                weight = jnp.exp2((score - new) * rate)
                fade = jnp.exp2((old - new) * rate)
                acc[at, :] = acc[at, :] * fade + pair_dot(weight.astype(jnp.bfloat16), values)
            top[at, :] = jnp.broadcast_to(new, (tile, width))

    attend(k_ref, v_ref, me_k, True)
    arrived(kbuf.at[0], kv_send.at[0], kv_recv.at[0])
    arrived(vbuf.at[0], kv_send.at[1], kv_recv.at[1])
    attend(kbuf.at[0], vbuf.at[0], x * 2 + 1 - core, False)

    for o in range(1, n_flat):
        block = place(behind(o), core)
        arrived(slots.at[block], sl_send.at[o], sl_recv.at[o])
        i = n_flat - 1 + o
        send(slots.at[block], slots.at[block], sl_send.at[i], sl_recv.at[i], sibling)
    arrived(slots.at[place(flat, 1 - core)], sl_send.at[0], sl_recv.at[0])
    for o in range(1, n_flat):
        i = n_flat - 1 + o
        arrived(slots.at[place(behind(o), 1 - core)], sl_send.at[i], sl_recv.at[i])

    def slot_keys():
        return slots[:, :, 0:width].reshape(n_slots, width)

    def slot_values():
        return slots[:, :, width:].reshape(n_slots, width)

    def grouped(value):
        return value.reshape(slots.shape[0], per, tile)

    values_t = slot_values().astype(jnp.float32).T.astype(jnp.bfloat16)

    for t in range(tiles):
        at = pl.ds(t * tile, tile)
        score = row_scores(slot_keys(), q_ref[at, :])
        peak = jnp.max(score, axis=0, keepdims=True)
        weight = jnp.exp2((score - peak) * rate)
        prob = weight * (1.0 / jnp.sum(weight, axis=0, keepdims=True))
        e_ref[:, :, at] = grouped(prob)
        prob_b = prob.astype(jnp.bfloat16)
        pb_ref[:, :, at] = grouped(prob_b)
        student[at, :] = pair_dot(values_t, prob_b).T

    for j in range(1, n_x):
        s = 2 * j - 1
        arrived(kbuf.at[s], kv_send.at[2 * s], kv_recv.at[2 * s])
        arrived(vbuf.at[s], kv_send.at[2 * s + 1], kv_recv.at[2 * s + 1])
        g = s + 1
        send(kbuf.at[s], kbuf.at[g], kv_send.at[2 * g], kv_recv.at[2 * g], sibling)
        send(vbuf.at[s], vbuf.at[g], kv_send.at[2 * g + 1], kv_recv.at[2 * g + 1], sibling)
    for j in range(1, n_x):
        far = lax.rem(x + n_x - j, n_x) * 2
        s = 2 * j - 1
        attend(kbuf.at[s], vbuf.at[s], far + core, False)
        g = s + 1
        arrived(kbuf.at[g], kv_send.at[2 * g], kv_recv.at[2 * g])
        arrived(vbuf.at[g], kv_send.at[2 * g + 1], kv_recv.at[2 * g + 1])
        attend(kbuf.at[g], vbuf.at[g], far + 1 - core, False)

    sq_own[...] = jnp.zeros_like(sq_own)
    for t in range(tiles):
        at = pl.ds(t * tile, tile)
        teacher = (acc[at, 0:width] / acc[at, width:]).astype(jnp.bfloat16)
        teach_ref[at, :] = teacher
        diff = student[at, :] - teacher.astype(jnp.float32)
        sq_own[...] += jnp.sum((diff * diff).reshape(tile // 8, 8, width), axis=0)
        diffb[at, :] = diff.astype(jnp.bfloat16)
    write_teach = pltpu.make_async_copy(teach_ref, teach_hbm, out_sem.at[0])
    write_teach.start()
    send(sq_own, sq_sib, sq_send.at[0], sq_recv.at[0], sibling)

    order = list(range(1, n_flat)) + [0]
    group = 2 if n_flat % 2 == 0 else 1
    batches = n_flat // group
    VALUES, KEYS = 0, 1

    def produce(half, i):
        left, right = ((pb_ref, diffb), (ds_ref, q_ref))[half]
        first = i * group
        offsets = order[first:first + group]
        blocks = [place(ahead(o), 1 - core) for o in offsets]
        blocks += [place(ahead(o), core) for o in offsets]
        terms = pair_dot(jnp.concatenate([left[b] for b in blocks], axis=0), right[...])
        terms = terms.reshape(2, group, per, width)
        span = pl.ds(first, group)
        gsib_out[half, span] = terms[0]
        gmine[half, span] = terms[1]
        sem = half * batches + i
        send(gsib_out.at[half, span], gsib_in.at[half, span], gs_send.at[sem], gs_recv.at[sem], sibling)

    def finish(half, i):
        first = i * group
        sem = half * batches + i
        arrived(gsib_in.at[half, pl.ds(first, group)], gs_send.at[sem], gs_recv.at[sem])
        for p in range(first, first + group):
            o = order[p]
            if o > 0:
                gout[half, p] = (gmine[half, p] + gsib_in[half, p]).astype(jnp.bfloat16)
                i = half * n_flat + p
                send(gout.at[half, p], gin.at[half, p], g_send.at[i], g_recv.at[i], peer(ahead(o)))

    for i in range(batches):
        produce(VALUES, i)

    for t in range(tiles):
        at = pl.ds(t * tile, tile)
        dprob = row_scores(slot_values(), diffb[at, :])
        prob = e_ref[:, :, at].reshape(n_slots, tile)
        inner = jnp.sum(prob * dprob, axis=0, keepdims=True)
        ds_ref[:, :, at] = grouped((prob * (dprob - inner) * scale).astype(jnp.bfloat16))
        if t == 0:
            for i in range(batches):
                finish(VALUES, i)
            arrived(sq_sib, sq_send.at[0], sq_recv.at[0])
            sq_chip[...] = sq_own[...] + sq_sib[...]
            for o in range(1, n_flat):
                send(sq_chip, sq_in.at[o], sq_send.at[o], sq_recv.at[o], peer(ahead(o)))

    for i in range(batches):
        produce(KEYS, i)
        if i > 1:
            finish(KEYS, i - 2)
    for i in range(max(batches - 2, 0), batches):
        finish(KEYS, i)

    squares = sq_chip[...]
    for o in range(1, n_flat):
        arrived(sq_in.at[o], sq_send.at[o], sq_recv.at[o])
        squares = squares + sq_in[o]
    loss = jnp.sum(squares, keepdims=True) * (1.0 / (rows * n_keys * n_qry))
    loss_ref[...] = jnp.broadcast_to(loss, loss_ref.shape)
    write_loss = pltpu.make_async_copy(loss_ref, loss_hbm, out_sem.at[2])
    write_loss.start()
    for load in loads[4:]:
        load.wait()
    for half in (VALUES, KEYS):
        total = gmine[half, n_flat - 1] + gsib_in[half, n_flat - 1]
        for p in range(n_flat - 1):
            i = half * n_flat + p
            arrived(gin.at[half, p], g_send.at[i], g_recv.at[i])
            total = total + gin[half, p].astype(jnp.float32)
        part = pl.ds(width if half == VALUES else 0, width)
        new_first = 0.9 * first_ref[:, part] + 0.1 * total
        new_second = 0.95 * second_ref[:, part] + 0.05 * total * total
        owned_ref[0, :, part] = total
        owned_ref[1, :, part] = slot_ref[:, part] - 0.02 * new_first / (jnp.sqrt(new_second) + 1e-08)
        owned_ref[2, :, part] = new_first
        owned_ref[3, :, part] = new_second
    write_owned = pltpu.make_async_copy(owned_ref, owned_hbm, out_sem.at[1])
    write_owned.start()
    write_teach.wait()
    write_owned.wait()
    write_loss.wait()
    for copy in pending:
        copy.wait_send()


def write_kernel(
    teach_hbm, owned_hbm, loss_hbm, teach_out, grad_out, params_out, first_out, second_out, loss_out,
    teach, owned, loss, sems,
):
    loads = [
        pltpu.make_async_copy(src, dst, sems.at[i])
        for i, (src, dst) in enumerate(((owned_hbm, owned), (teach_hbm, teach), (loss_hbm, loss)))
    ]
    for load in loads:
        load.start()
    loads[0].wait()
    copies = [
        pltpu.make_async_copy(owned.at[i], out, sems.at[3 + i])
        for i, out in enumerate((grad_out, params_out, first_out, second_out))
    ]
    for copy in copies:
        copy.start()
    loads[1].wait()
    copies.append(pltpu.make_async_copy(teach, teach_out, sems.at[7]))
    copies[4].start()
    loads[2].wait()
    loss_out[0] = jnp.max(loss[...])
    for copy in copies:
        copy.wait()


def fused(
    queries, cache_keys, cache_values, entry, visits, doc_length, slot_params,
    first_moment, second_moment,
):
    n_keys = lax.axis_size("keys")
    n_qry = lax.axis_size("qry")
    n_flat = n_keys // 2 * n_qry
    n_blocks = n_keys * n_qry
    tok, heads, width = queries.shape
    rows = tok * heads
    per, wide = slot_params.shape
    shard_len = cache_keys.shape[0]
    n_slots = per * n_blocks
    f32, bf16 = jnp.float32, jnp.bfloat16
    hbm = pl.BlockSpec(memory_space=pltpu.HBM)
    smem = pl.BlockSpec(memory_space=pltpu.SMEM)
    dma = pltpu.SemaphoreType.DMA
    owned = jax.ShapeDtypeStruct((per, wide), f32)
    flops = 2 * rows * width * (2 * n_keys * shard_len + 5 * n_slots)
    teach, stacked, loss = pl.pallas_call(
        functools.partial(step_kernel, n_keys, n_qry),
        out_shape=(
            jax.ShapeDtypeStruct((rows, width), bf16),
            jax.ShapeDtypeStruct((4, per, wide), f32),
            jax.ShapeDtypeStruct((8, width), f32),
        ),
        in_specs=[smem] * 3 + [hbm] * 6,
        out_specs=(hbm,) * 3,
        scratch_shapes=[
            pltpu.VMEM((rows, width), bf16),
            pltpu.VMEM((4, per, wide), f32),
            pltpu.VMEM((8, width), f32),
            pltpu.VMEM((rows, width), bf16),
            pltpu.VMEM((shard_len, width), bf16),
            pltpu.VMEM((shard_len, width), bf16),
            pltpu.VMEM((per, wide), f32),
            pltpu.VMEM((per, wide), f32),
            pltpu.VMEM((per, wide), f32),
            pltpu.VMEM((n_keys - 1, shard_len, width), bf16),
            pltpu.VMEM((n_keys - 1, shard_len, width), bf16),
            pltpu.VMEM((n_blocks, per, wide), bf16),
            pltpu.VMEM((rows, width), f32),
            pltpu.VMEM((rows, 2 * width), f32),
            pltpu.VMEM((n_blocks, per, rows), f32),
            pltpu.VMEM((n_blocks, per, rows), bf16),
            pltpu.VMEM((n_blocks, per, rows), bf16),
            pltpu.VMEM((rows, width), f32),
            pltpu.VMEM((rows, width), bf16),
            pltpu.VMEM((2, n_flat, per, width), f32),
            pltpu.VMEM((2, n_flat, per, width), f32),
            pltpu.VMEM((2, n_flat, per, width), f32),
            pltpu.VMEM((2, n_flat, per, width), bf16),
            pltpu.VMEM((2, n_flat, per, width), bf16),
            pltpu.VMEM((8, width), f32),
            pltpu.VMEM((8, width), f32),
            pltpu.VMEM((8, width), f32),
            pltpu.VMEM((n_flat, 8, width), f32),
            dma((6,)),
            dma((3,)),
            dma((2 * (n_keys - 1),)),
            dma((2 * (n_keys - 1),)),
            dma((2 * n_flat - 1,)),
            dma((2 * n_flat - 1,)),
            dma((2 * n_flat,)),
            dma((2 * n_flat,)),
            dma((2 * n_flat,)),
            dma((2 * n_flat,)),
            dma((n_flat,)),
            dma((n_flat,)),
        ],
        compiler_params=pltpu.CompilerParams(
            collective_id=0, has_side_effects=True, vmem_limit_bytes=63 * 2**20
        ),
        cost_estimate=pl.CostEstimate(
            flops=flops, bytes_accessed=4 * rows * width, transcendentals=rows * n_slots
        ),
    )(
        entry, visits, doc_length, queries.reshape(rows, width), cache_keys, cache_values,
        slot_params, first_moment, second_moment,
    )
    out = pl.pallas_call(
        write_kernel,
        out_shape=(
            jax.ShapeDtypeStruct((rows, width), bf16), owned, owned, owned, owned,
            jax.ShapeDtypeStruct((1,), f32),
        ),
        in_specs=[hbm] * 3,
        out_specs=(hbm,) * 5 + (smem,),
        scratch_shapes=[
            pltpu.VMEM((rows, width), bf16),
            pltpu.VMEM((4, per, wide), f32),
            pltpu.VMEM((8, width), f32),
            dma((8,)),
        ],
        compiler_params=pltpu.CompilerParams(vmem_limit_bytes=63 * 2**20),
    )(teach, stacked, loss)
    return (out[0].reshape(tok, heads, width),) + tuple(out[1:])


def body(*args):
    per = args[6].shape[0]
    if per % 16 == 0 and lax.axis_size("keys") % 2 == 0:
        return fused(*args)
    return ringed(*args)


def solution(mesh):
    return jax.shard_map(
        body,
        mesh=mesh,
        in_specs=(
            P(("grp", "keys", "qry"), None, None),
            P(("grp", "keys"), None),
            P(("grp", "keys"), None),
            P(("grp", "keys"), "qry"),
            P(("grp", "keys"), "qry"),
            P("grp"),
            P(("grp", "keys", "qry"), None),
            P(("grp", "keys", "qry"), None),
            P(("grp", "keys", "qry"), None),
        ),
        out_specs=(
            P(("grp", "keys", "qry"), None, None),
            P(("grp", "keys", "qry"), None),
            P(("grp", "keys", "qry"), None),
            P(("grp", "keys", "qry"), None),
            P(("grp", "keys", "qry"), None),
            P("grp"),
        ),
        check_vma=False,
    )
```
